32 devices in a mesh: slab: 8 (over z, y), chan: 4 (over x, core).
Axes of the slice: x: 2, y: 2, z: 4, core: 2. Of those that a mesh axis runs over, the one named last changes fastest.
Arguments:
- field: bfloat16 [64, 256, 4096], P(None, 'slab'), may hold values from -6 to 6
- cotangent: bfloat16 [64, 256, 4096], P(None, 'slab'), may hold values from -10 to 10
- spectral_weight: bfloat16 [2, 64, 64, 512, 32], P(None, 'chan', None, 'slab'), may hold values from -4 to 4
- point_weight: bfloat16 [64, 64], replicated, may hold values from -0.75 to 0.75
- point_bias: bfloat16 [64], replicated, may hold values from -2 to 2
Outputs:
- grad_input: bfloat16 [64, 256, 4096], P('chan', 'slab')
- grad_spectral: float32 [2, 64, 64, 512, 32], P(None, 'chan', None, 'slab')
- grad_pointwise: float32 [64, 64], P('chan')
- grad_bias: float32 [64], replicated
The draws below stay inside these ranges and needn't reach their ends.
All inputs are finite; a program needn't handle non-finite values.
Results may differ from the reference program's by a relative error of at most 0.023.
Values may be sent and summed in bfloat16 or wider, within the bound.
A program may use at most 256 MiB of HBM per device.

```python
import math
import jax
import jax.numpy as jnp
from jax import lax

C = 64
MX = 32
MY = 32
MZ = 16
NX = 256
NY = 64
NZ = 64
MODES = 512


def draw_cotangent(key, part):
    noise_key = jax.random.fold_in(key, 11)
    positions = jnp.arange(NX, dtype=jnp.float32) / (NX - 1)
    base_noise = jnp.clip(jax.random.normal(noise_key, (C, NX, NY * NZ), jnp.float32), -6.0, 6.0)
    plane_ramp = 0.5 + positions
    scaled = base_noise * plane_ramp[None, :, None]
    return scaled.astype(jnp.bfloat16)


def block_levels(stream_key, shape, split, least, largest):
    loudness = 1.0
    for dim, shards_of in split:
        steps = jax.random.uniform(jax.random.fold_in(jax.random.fold_in(stream_key, 6), dim), (shards_of,), jnp.float32, least / len(split), largest / len(split))
        loudness = loudness * jnp.repeat(jnp.exp(steps), shape[dim] // shards_of).reshape((-1,) + (1,) * (len(shape) - 1 - dim))
    return loudness


def noise(stream_key, extent, scale, reach, cuts=(), kind=jnp.bfloat16):
    loudness = block_levels(stream_key, extent, cuts, -0.22, 0.18) if cuts else 1.0
    array = jax.random.normal(stream_key, extent, jnp.float32) * scale * loudness
    return jnp.minimum(jnp.maximum(array, -reach), reach).astype(kind)


def setup_inputs(seed: int = 0) -> dict:
    key_list = jax.random.split(jax.random.key(seed), 6)
    return {
        "field": noise(key_list[0], (C, NX, NY * NZ), 1.0, 6.0, ((1, 8),)),
        "cotangent": draw_cotangent(jax.random.fold_in(key_list[5], 71), 0),
        "spectral_weight": noise(key_list[2], (2, C, C, MODES, MX), 0.7, 4.0, ((1, 4), (3, 8))),
        "point_weight": noise(key_list[3], (C, C), C ** -0.5, 0.75),
        "point_bias": noise(key_list[4], (C,), 0.5, 2.0),
    }


def kept_modes(total, length):
    mode_index = jnp.arange(total, dtype=jnp.int32)
    return jnp.where(mode_index < total // 2, mode_index, mode_index - total + length)

def phases(frequency, length):
    positions = jnp.arange(length, dtype=jnp.int32)
    wound_up = frequency[:, None] * positions[None, :] % length
    return 2.0 * math.pi / length * wound_up.astype(jnp.float32)

def make_tables():
    angle_z = phases(jnp.arange(MZ, dtype=jnp.int32), NZ)
    cosine_z = jnp.cos(angle_z)
    sine_z = jnp.sin(angle_z)
    forward_z = jnp.stack([cosine_z.T, -sine_z.T], 1).astype(jnp.bfloat16)
    weight_z = (jnp.where(jnp.arange(MZ) == 0, 1.0, 2.0) / (NX * NY * NZ)).astype(jnp.float32)
    scaled_z = jnp.stack([weight_z[:, None] * cosine_z, -weight_z[:, None] * sine_z], 1).astype(jnp.bfloat16)
    plain_z = jnp.stack([cosine_z, -sine_z], 1).astype(jnp.bfloat16)
    angle_y = phases(kept_modes(MY, NY), NY)
    cosine_y = jnp.cos(angle_y)
    sine_y = jnp.sin(angle_y)
    upper_rows = jnp.stack([cosine_y.T, -sine_y.T], -1)
    lower_rows = jnp.stack([sine_y.T, cosine_y.T], -1)
    forward_y = jnp.stack([upper_rows, lower_rows], 0).reshape(2 * NY, 2 * MY).astype(jnp.bfloat16)
    real_rows = jnp.stack([cosine_y, sine_y], 1)
    imag_rows = jnp.stack([-sine_y, cosine_y], 1)
    inverse_y = jnp.stack([real_rows, imag_rows], 1).reshape(2 * MY, 2 * NY).astype(jnp.bfloat16)
    angle_x = phases(kept_modes(MX, NX), NX)
    cosine_x = jnp.cos(angle_x).T.astype(jnp.bfloat16)
    sine_x = jnp.sin(angle_x).T.astype(jnp.bfloat16)
    return (forward_z, scaled_z, plain_z, forward_y, inverse_y, cosine_x, sine_x)

def product(form, left, right):
    return jnp.einsum(form, left.astype(jnp.float32), right.astype(jnp.float32), precision=lax.Precision.HIGHEST)

def to_modes(field_part, tables):
    forward_z, scaled_z, plain_z, forward_y, inverse_y, cosine_x, sine_x = tables
    channels = field_part.shape[0]
    grid_view = field_part.reshape(channels, NX, NY, NZ)
    section_one = product('cxyz,zpk->cxkpy', grid_view, forward_z).astype(jnp.bfloat16)
    section_one = section_one.reshape(channels, NX, MZ, 2 * NY)
    section_two = product('cxkm,mn->cxkn', section_one, forward_y).astype(jnp.bfloat16)
    pencils = section_two.reshape(channels, NX, MODES, 2)
    along_cos = product('cxmq,xk->cmqk', pencils, cosine_x)
    along_sin = product('cxmq,xk->cmqk', pencils, sine_x)
    real_part = along_cos[:, :, 0] + along_sin[:, :, 1]
    imag_part = along_cos[:, :, 1] - along_sin[:, :, 0]
    return jnp.stack([real_part, imag_part], 2)

def to_grid(spectra, tables, table_z):
    forward_z, scaled_z, plain_z, forward_y, inverse_y, cosine_x, sine_x = tables
    channels = spectra.shape[0]
    back_cos = product('cmqk,xk->cxmq', spectra, cosine_x)
    back_sin = product('cmqk,xk->cxmq', spectra, sine_x)
    real_part = back_cos[..., 0] - back_sin[..., 1]
    imag_part = back_cos[..., 1] + back_sin[..., 0]
    pencil_rows = jnp.stack([real_part, imag_part], -1).astype(jnp.bfloat16)
    slabs = pencil_rows.reshape(channels, NX, MZ, 2 * MY)
    section_two = product('cxkn,nm->cxkm', slabs, inverse_y).astype(jnp.bfloat16)
    section_two = section_two.reshape(channels, NX, MZ, 2, NY)
    grid_view = product('cxkpy,kpz->cxyz', section_two, table_z)
    return grid_view.reshape(channels, NX, NY * NZ)

def gelu_grad(pre_act):
    normal_cdf = 0.5 * (1.0 + jax.scipy.special.erf(pre_act / math.sqrt(2.0)))
    normal_pdf = jnp.exp(-0.5 * pre_act * pre_act) / math.sqrt(2.0 * math.pi)
    return normal_cdf + pre_act * normal_pdf

def reference(field, cotangent, spectral_weight, point_weight, point_bias):
    tables = make_tables()
    scaled_z = tables[1]
    plain_z = tables[2]
    coeff = to_modes(field, tables).astype(jnp.bfloat16)
    coeff_real = coeff[:, :, 0].astype(jnp.float32)
    coeff_imag = coeff[:, :, 1].astype(jnp.float32)
    real_weight = spectral_weight[0].astype(jnp.float32)
    imag_weight = spectral_weight[1].astype(jnp.float32)
    spec_real = product('imk,iomk->omk', coeff_real, real_weight) - product('imk,iomk->omk', coeff_imag, imag_weight)
    spec_imag = product('imk,iomk->omk', coeff_real, imag_weight) + product('imk,iomk->omk', coeff_imag, real_weight)
    spectra = jnp.stack([spec_real, spec_imag], 2)
    shaped = to_grid(spectra.astype(jnp.bfloat16), tables, scaled_z)
    pre_act = shaped + product('io,ixc->oxc', point_weight, field) + point_bias.astype(jnp.float32)[:, None, None]
    grad_pre = (cotangent.astype(jnp.float32) * gelu_grad(pre_act)).astype(jnp.bfloat16)
    mode_index = jnp.arange(MODES, dtype=jnp.int32)
    mode_scale = (jnp.where(mode_index // MY == 0, 1.0, 2.0) / (NX * NY * NZ)).astype(jnp.float32)
    grad_hat = (to_modes(grad_pre, tables) * mode_scale[None, :, None, None]).astype(jnp.bfloat16)
    grad_real = grad_hat[:, :, 0].astype(jnp.float32)
    grad_imag = grad_hat[:, :, 1].astype(jnp.float32)

    def one_row(row_pair):
        row_real, row_imag = row_pair
        part_real = row_real[None] * grad_real + row_imag[None] * grad_imag
        part_imag = row_real[None] * grad_imag - row_imag[None] * grad_real
        return jnp.stack([part_real, part_imag], 0)
    grad_spectral = jnp.moveaxis(lax.map(one_row, (coeff_real, coeff_imag)), 0, 1)
    adj_real = product('omk,iomk->imk', grad_real, real_weight) + product('omk,iomk->imk', grad_imag, imag_weight)
    adj_imag = product('omk,iomk->imk', grad_imag, real_weight) - product('omk,iomk->imk', grad_real, imag_weight)
    adjoint = jnp.stack([adj_real, adj_imag], 2).astype(jnp.bfloat16)
    spectral_back = to_grid(adjoint, tables, plain_z)
    grad_input = (spectral_back + product('io,oxc->ixc', point_weight, grad_pre)).astype(jnp.bfloat16)
    inverse_root = 1.0 / math.sqrt(NX * NY * NZ)
    grad_pointwise = product('ixc,oxc->io', field, grad_pre) * inverse_root
    grad_bias = lax.optimization_barrier(jnp.sum(grad_pre.astype(jnp.float32), axis=(1, 2))) * inverse_root
    return (grad_input, grad_spectral, grad_pointwise, grad_bias)
```

```python
import functools
import math

import jax
import jax.numpy as jnp
import ml_dtypes
import numpy as np
from jax import lax
from jax.experimental import pallas as pl
from jax.experimental.pallas import tpu as pltpu
from jax.sharding import PartitionSpec as P

MX = 32
MY = 32
MZ = 16
NY = 64
NZ = 64

BF16 = ml_dtypes.bfloat16
VMEM_LIMIT = 50 * 1024 * 1024


def kept_modes(total, length):
    mode_index = np.arange(total, dtype=np.int32)
    return np.where(mode_index < total // 2, mode_index, mode_index - total + length)


def rounded_waves(frequency, length):
    positions = np.arange(length, dtype=np.int32)
    wound_up = frequency[:, None] * positions[None, :] % length
    angle = np.float32(2.0 * math.pi / length) * wound_up.astype(np.float32)
    cosine = np.cos(angle).astype(BF16).astype(np.float32)
    sine = np.sin(angle).astype(BF16).astype(np.float32)
    return cosine, sine


def plane_table(slabs):
    cosine_z, sine_z = rounded_waves(np.arange(MZ, dtype=np.int32), NZ)
    cosine_y, sine_y = rounded_waves(kept_modes(MY, NY), NY)
    cz, sz = cosine_z.T[None, :, :, None], sine_z.T[None, :, :, None]
    cy, sy = cosine_y.T[:, None, None, :], sine_y.T[:, None, None, :]
    real = (cz * cy - sz * sy).reshape(NY * NZ, slabs, 1, -1)
    imag = -(cz * sy + sz * cy).reshape(NY * NZ, slabs, 1, -1)
    return np.concatenate([real, imag], 2).reshape(NY * NZ, -1).astype(BF16)


def line_tables(length):
    cosine, sine = rounded_waves(kept_modes(MX, length), length)
    return cosine.astype(BF16), sine.astype(BF16)


def gelu_grad(pre_act):
    normal_cdf = 0.5 * (1.0 + lax.erf(pre_act * (1.0 / math.sqrt(2.0))))
    normal_pdf = jnp.exp(-0.5 * pre_act * pre_act) * (1.0 / math.sqrt(2.0 * math.pi))
    return normal_cdf + pre_act * normal_pdf


def params():
    return pltpu.CompilerParams(vmem_limit_bytes=VMEM_LIMIT)


def pick(total, wanted):
    return math.gcd(total, wanted)


def mix_kernel(coeff_ref, weight_ref, out_ref, *, inner):
    group, outs = weight_ref.shape[1], weight_ref.shape[2]
    shape = weight_ref.shape[3:]

    def some_outputs(step, carry):
        first = step * inner

        def one_input(i, sums):
            real, imag = coeff_ref[i, 0], coeff_ref[i, 1]
            done = []
            for k in range(inner):
                wr = weight_ref[0, i, first + k].astype(jnp.float32)
                wi = weight_ref[1, i, first + k].astype(jnp.float32)
                done.append(sums[2 * k] + (real * wr - imag * wi))
                done.append(sums[2 * k + 1] + (real * wi + imag * wr))
            return tuple(done)

        zero = jnp.zeros(shape, jnp.float32)
        sums = lax.fori_loop(0, group, one_input, (zero,) * (2 * inner), unroll=2)
        for k in range(inner):
            out_ref[first + k, 0] = sums[2 * k].astype(out_ref.dtype)
            out_ref[first + k, 1] = sums[2 * k + 1].astype(out_ref.dtype)
        return carry

    lax.fori_loop(0, outs // inner, some_outputs, 0)


def mix(coeff, weight):
    group, channels, lines, modes = weight.shape[1:]
    block = pick(channels, 8)
    return pl.pallas_call(
        functools.partial(mix_kernel, inner=pick(block, 4)),
        grid=(channels // block,),
        in_specs=[
            pl.BlockSpec((group, 2, lines, modes), lambda s: (0, 0, 0, 0)),
            pl.BlockSpec((2, group, block, lines, modes), lambda s: (0, 0, s, 0, 0)),
        ],
        out_specs=pl.BlockSpec((block, 2, lines, modes), lambda s: (s, 0, 0, 0)),
        out_shape=jax.ShapeDtypeStruct((channels, 2, lines, modes), jnp.bfloat16),
        compiler_params=params(),
        cost_estimate=pl.CostEstimate(
            flops=8 * weight.size // 2, bytes_accessed=4 * weight.size, transcendentals=0
        ),
        name="mix",
    )(coeff, weight)


def adjoint_kernel(hat_ref, weight_ref, out_ref, *, inner):
    own, channels = weight_ref.shape[1], weight_ref.shape[2]
    shape = weight_ref.shape[3:]
    for first in range(0, own, inner):

        def one_output(o, sums):
            real, imag = hat_ref[o, 0], hat_ref[o, 1]
            done = []
            for k in range(inner):
                wr = weight_ref[0, first + k, o].astype(jnp.float32)
                wi = weight_ref[1, first + k, o].astype(jnp.float32)
                done.append(sums[2 * k] + (real * wr + imag * wi))
                done.append(sums[2 * k + 1] + (imag * wr - real * wi))
            return tuple(done)

        zero = jnp.zeros(shape, jnp.float32)
        sums = lax.fori_loop(0, channels, one_output, (zero,) * (2 * inner), unroll=2)
        for k in range(inner):
            out_ref[first + k, 0] = sums[2 * k].astype(out_ref.dtype)
            out_ref[first + k, 1] = sums[2 * k + 1].astype(out_ref.dtype)


def adjoint_of(hat, weight):
    group, channels, lines, modes = weight.shape[1:]
    block = pick(group, 2)
    return pl.pallas_call(
        functools.partial(adjoint_kernel, inner=block),
        grid=(group // block,),
        in_specs=[
            pl.BlockSpec((channels, 2, lines, modes), lambda s: (0, 0, 0, 0)),
            pl.BlockSpec((2, block, channels, lines, modes), lambda s: (0, s, 0, 0, 0)),
        ],
        out_specs=pl.BlockSpec((block, 2, lines, modes), lambda s: (s, 0, 0, 0)),
        out_shape=jax.ShapeDtypeStruct((group, 2, lines, modes), jnp.bfloat16),
        compiler_params=params(),
        cost_estimate=pl.CostEstimate(
            flops=8 * weight.size // 2, bytes_accessed=4 * weight.size, transcendentals=0
        ),
        name="adjoint",
    )(hat, weight)


def outer_kernel(coeff_ref, hat_ref, out_ref):
    own, channels = out_ref.shape[1], out_ref.shape[2]
    for i in range(own):
        cr, ci = coeff_ref[i, 0], coeff_ref[i, 1]

        def one_output(o, carry):
            hr, hi = hat_ref[o, 0], hat_ref[o, 1]
            out_ref[0, i, o] = cr * hr + ci * hi
            out_ref[1, i, o] = cr * hi - ci * hr
            return carry

        lax.fori_loop(0, channels, one_output, 0, unroll=4)


def outer(coeff, hat):
    group, _, lines, modes = coeff.shape
    channels = hat.shape[0]
    block = pick(group, 2)
    return pl.pallas_call(
        outer_kernel,
        grid=(group // block,),
        in_specs=[
            pl.BlockSpec((block, 2, lines, modes), lambda s: (s, 0, 0, 0)),
            pl.BlockSpec((channels, 2, lines, modes), lambda s: (0, 0, 0, 0)),
        ],
        out_specs=pl.BlockSpec((2, block, channels, lines, modes), lambda s: (0, s, 0, 0, 0)),
        out_shape=jax.ShapeDtypeStruct((2, group, channels, lines, modes), jnp.float32),
        compiler_params=params(),
        cost_estimate=pl.CostEstimate(
            flops=6 * group * channels * lines * modes,
            bytes_accessed=16 * group * channels * lines * modes,
            transcendentals=0,
        ),
        name="outer",
    )(coeff, hat)


ROWS_BY_ROWS = (((1,), (1,)), ((), ()))


def grid_kernel(
    modes_ref, table_ref, field_ref, cotangent_ref, mix_ref, back_ref, bias_ref,
    point_ref, hat_ref, weight_ref, sum_ref, total,
):
    step = pl.program_id(0)

    @pl.when(step == 0)
    def _():
        total[...] = jnp.zeros_like(total)
        weight_ref[...] = jnp.zeros_like(weight_ref)
        sum_ref[...] = jnp.zeros_like(sum_ref)

    table = table_ref[...]
    field = field_ref[...]
    pre_act = lax.dot_general(
        modes_ref[...], table, ROWS_BY_ROWS, preferred_element_type=jnp.float32
    )
    pre_act += jnp.dot(mix_ref[...], field, preferred_element_type=jnp.float32)
    pre_act += bias_ref[...]
    grad_wide = cotangent_ref[...].astype(jnp.float32) * gelu_grad(pre_act)
    grad_pre = grad_wide.astype(jnp.bfloat16)
    point_ref[...] = jnp.dot(
        back_ref[...], grad_pre, preferred_element_type=jnp.float32
    ).astype(point_ref.dtype)
    total[...] += jnp.dot(grad_pre, table, preferred_element_type=jnp.float32)
    weight_ref[...] += lax.dot_general(
        field, grad_pre, ROWS_BY_ROWS, preferred_element_type=jnp.float32
    )
    sum_ref[...] += jnp.sum(grad_pre.astype(jnp.float32), axis=1, keepdims=True)

    @pl.when(step == pl.num_programs(0) - 1)
    def _():
        hat_ref[...] = total[...].astype(hat_ref.dtype)


def grid_stage(modes, table, field, cotangent, mixing, backing, bias):
    rows, width = modes.shape
    cells = table.shape[0]
    block = pick(cells, 512)
    still = lambda s: (0, 0)
    along = lambda s: (0, s)
    return pl.pallas_call(
        grid_kernel,
        grid=(cells // block,),
        in_specs=[
            pl.BlockSpec((rows, width), still),
            pl.BlockSpec((block, width), lambda s: (s, 0)),
            pl.BlockSpec((rows, block), along),
            pl.BlockSpec((rows, block), along),
            pl.BlockSpec((rows, rows), still),
            pl.BlockSpec((rows, rows), still),
            pl.BlockSpec((rows, 1), still),
        ],
        out_specs=[
            pl.BlockSpec((rows, block), along),
            pl.BlockSpec((rows, width), still),
            pl.BlockSpec((rows, rows), still),
            pl.BlockSpec((rows, 1), still),
        ],
        out_shape=[
            jax.ShapeDtypeStruct((rows, cells), jnp.bfloat16),
            jax.ShapeDtypeStruct((rows, width), jnp.bfloat16),
            jax.ShapeDtypeStruct((rows, rows), jnp.float32),
            jax.ShapeDtypeStruct((rows, 1), jnp.float32),
        ],
        scratch_shapes=[pltpu.VMEM((rows, width), jnp.float32)],
        compiler_params=params(),
        cost_estimate=pl.CostEstimate(
            flops=2 * rows * cells * (2 * width + 3 * rows),
            bytes_accessed=2 * cells * (width + 3 * rows),
            transcendentals=2 * rows * cells,
        ),
        name="grid",
    )(modes, table, field, cotangent, mixing, backing, bias)


def pad_planes(array, dim, spare):
    if not spare:
        return array
    return jnp.pad(array, [(0, spare if d == dim else 0) for d in range(array.ndim)])


def line_modes(pencils, tables):
    cosine, sine = tables
    along_cos = jnp.einsum("cxqm,kx->cqkm", pencils, cosine, preferred_element_type=jnp.float32)
    along_sin = jnp.einsum("cxqm,kx->cqkm", pencils, sine, preferred_element_type=jnp.float32)
    real = along_cos[:, 0] + along_sin[:, 1]
    imag = along_cos[:, 1] - along_sin[:, 0]
    return jnp.stack([real, imag], 1)


def line_values(spectra, tables):
    cosine, sine = tables
    back_cos = jnp.einsum("cqkm,kx->cxqm", spectra, cosine, preferred_element_type=jnp.float32)
    back_sin = jnp.einsum("cqkm,kx->cxqm", spectra, sine, preferred_element_type=jnp.float32)
    real = back_cos[:, :, 0] - back_sin[:, :, 1]
    imag = back_cos[:, :, 1] + back_sin[:, :, 0]
    return jnp.stack([real, imag], 2)


def body(slabs, chans, field, cotangent, spectral_weight, point_weight, point_bias):
    channels, planes, cells = field.shape
    group = spectral_weight.shape[1]
    modes = spectral_weight.shape[3]
    own_planes = -(-planes // chans)
    spare = own_planes * chans - planes
    length = planes * slabs
    width = 2 * modes
    table = lax.optimization_barrier(jnp.asarray(plane_table(slabs)))
    tables = tuple(jnp.asarray(t) for t in line_tables(length))
    slab_index = lax.axis_index("slab")
    chan_index = lax.axis_index("chan")
    weight = jnp.swapaxes(spectral_weight, 3, 4)
    scale = 1.0 / (length * cells)
    mode_index = slab_index * modes + jnp.arange(modes, dtype=jnp.int32)
    mode_scale = (jnp.where(mode_index // MY == 0, 1.0, 2.0) * scale).astype(jnp.float32)

    own_field = lax.dynamic_slice_in_dim(field, chan_index * group, group, 0)
    sections = jnp.einsum(
        "rc,csn->srn",
        own_field.reshape(group * planes, cells),
        table.reshape(cells, slabs, width),
        preferred_element_type=jnp.float32,
    ).astype(jnp.bfloat16)
    pencils = lax.all_to_all(sections, "slab", split_axis=0, concat_axis=0, tiled=True)
    pencils = pencils.reshape(slabs, group, planes, 2, modes)
    pencils = jnp.moveaxis(pencils, 1, 0).reshape(group, length, 2, modes)
    coeff = line_modes(pencils, tables).astype(jnp.bfloat16).astype(jnp.float32)

    partial = mix(coeff, weight)
    spectra = lax.psum_scatter(partial, "chan", scatter_dimension=0, tiled=True)
    pencils = line_values(spectra, tables) * mode_scale
    pencils = pencils.astype(jnp.bfloat16).reshape(group, slabs, planes, width)
    pencils = pad_planes(pencils, 2, spare).reshape(group, slabs, chans, own_planes, width)
    pencils = jnp.transpose(pencils, (1, 2, 0, 3, 4))
    pencils = pencils.reshape(slabs * chans, group, own_planes, width)
    slabs_in = lax.all_to_all(
        pencils, ("slab", "chan"), split_axis=0, concat_axis=0, tiled=True
    )
    slabs_in = slabs_in.reshape(slabs, channels, own_planes, width)
    rows = channels * own_planes
    slabs_in = jnp.transpose(slabs_in, (1, 2, 0, 3)).reshape(rows, slabs * width)

    first_plane = chan_index * own_planes
    plane_field = lax.dynamic_slice_in_dim(
        pad_planes(field, 1, spare), first_plane, own_planes, 1
    )
    plane_cotangent = lax.dynamic_slice_in_dim(
        pad_planes(cotangent, 1, spare), first_plane, own_planes, 1
    )
    eye = jnp.eye(own_planes, dtype=jnp.bfloat16)
    point, hat_rows, weight_part, bias_part = grid_stage(
        slabs_in,
        table,
        plane_field.reshape(rows, cells),
        plane_cotangent.reshape(rows, cells),
        jnp.kron(point_weight.T, eye),
        jnp.kron(point_weight, eye),
        jnp.repeat(point_bias.astype(jnp.float32), own_planes)[:, None],
    )
    point = lax.all_to_all(
        point.reshape(chans, group, own_planes, cells),
        "chan", split_axis=0, concat_axis=0, tiled=True,
    )
    hat_rows = hat_rows.reshape(chans, group, own_planes, slabs, width)
    hat_rows = jnp.transpose(hat_rows, (3, 0, 1, 2, 4))
    hat_rows = hat_rows.reshape(slabs * chans, group, own_planes, width)
    pencils = lax.all_to_all(
        hat_rows, ("slab", "chan"), split_axis=0, concat_axis=0, tiled=True
    )
    pencils = jnp.moveaxis(pencils.reshape(slabs, chans, group, own_planes, width), 2, 0)
    pencils = pencils.reshape(group, slabs, chans * own_planes, width)[:, :, :planes]
    pencils = pencils.reshape(group, length, 2, modes)
    part_hat = (line_modes(pencils, tables) * mode_scale).astype(jnp.bfloat16)
    hat = lax.all_gather(part_hat, "chan", axis=0, tiled=True).astype(jnp.float32)

    adjoint = adjoint_of(hat, weight)
    grad_spectral = jnp.swapaxes(outer(coeff, hat), 3, 4)
    pencils = line_values(adjoint, tables).astype(jnp.bfloat16)
    pencils = pencils.reshape(group, slabs, planes, width)
    pencils = lax.all_to_all(
        jnp.moveaxis(pencils, 1, 0), "slab", split_axis=0, concat_axis=0, tiled=True
    )
    pencils = jnp.moveaxis(pencils, 0, 2).reshape(group * planes, slabs * width)
    back = lax.dot_general(pencils, table, ROWS_BY_ROWS, preferred_element_type=jnp.float32)
    back = back.reshape(group, planes, cells)
    point = jnp.moveaxis(point, 0, 1).reshape(group, chans * own_planes, cells)[:, :planes]
    grad_input = (back + point.astype(jnp.float32)).astype(jnp.bfloat16)

    inverse_root = 1.0 / math.sqrt(length * cells)
    weight_part = weight_part.reshape(channels, own_planes, channels, own_planes)
    weight_part = jnp.einsum("ipop->io", weight_part)
    bias_part = bias_part.reshape(channels, own_planes).sum(1)
    sums = jnp.concatenate([weight_part, bias_part[None]], 0) * inverse_root
    sums = lax.psum(sums, ("slab", "chan"))
    grad_pointwise = lax.dynamic_slice_in_dim(sums, chan_index * group, group, 0)
    return (grad_input, grad_spectral, grad_pointwise, sums[channels])


def solution(mesh):
    placed = (
        P(None, "slab", None),
        P(None, "slab", None),
        P(None, "chan", None, "slab", None),
        P(),
        P(),
    )
    return jax.shard_map(
        functools.partial(body, mesh.shape["slab"], mesh.shape["chan"]),
        mesh=mesh,
        in_specs=placed,
        out_specs=(
            P("chan", "slab", None),
            P(None, "chan", None, "slab", None),
            P("chan", None),
            P(),
        ),
        check_vma=False,
    )
```

```python
import functools
import math

import jax
import jax.numpy as jnp
import ml_dtypes
import numpy as np
from jax import lax
from jax.experimental import pallas as pl
from jax.experimental.pallas import tpu as pltpu
from jax.sharding import PartitionSpec as P

MX = 32
MY = 32
MZ = 16
NY = 64
NZ = 64

BF16 = ml_dtypes.bfloat16
VMEM_LIMIT = 50 * 1024 * 1024


def kept_modes(total, length):
    mode_index = np.arange(total, dtype=np.int32)
    return np.where(mode_index < total // 2, mode_index, mode_index - total + length)


def rounded_waves(frequency, length):
    positions = np.arange(length, dtype=np.int32)
    wound_up = frequency[:, None] * positions[None, :] % length
    angle = np.float32(2.0 * math.pi / length) * wound_up.astype(np.float32)
    cosine = np.cos(angle).astype(BF16).astype(np.float32)
    sine = np.sin(angle).astype(BF16).astype(np.float32)
    return cosine, sine


def plane_table(slabs):
    cosine_z, sine_z = rounded_waves(np.arange(MZ, dtype=np.int32), NZ)
    cosine_y, sine_y = rounded_waves(kept_modes(MY, NY), NY)
    cz, sz = cosine_z.T[None, :, :, None], sine_z.T[None, :, :, None]
    cy, sy = cosine_y.T[:, None, None, :], sine_y.T[:, None, None, :]
    real = (cz * cy - sz * sy).reshape(NY * NZ, slabs, 1, -1)
    imag = -(cz * sy + sz * cy).reshape(NY * NZ, slabs, 1, -1)
    return np.concatenate([real, imag], 2).reshape(NY * NZ, -1).astype(BF16)


def line_tables(length):
    cosine, sine = rounded_waves(kept_modes(MX, length), length)
    return cosine.astype(BF16), sine.astype(BF16)


def gelu_grad(pre_act):
    normal_cdf = 0.5 * (1.0 + lax.erf(pre_act * (1.0 / math.sqrt(2.0))))
    normal_pdf = jnp.exp(-0.5 * pre_act * pre_act) * (1.0 / math.sqrt(2.0 * math.pi))
    return normal_cdf + pre_act * normal_pdf


def params():
    return pltpu.CompilerParams(vmem_limit_bytes=VMEM_LIMIT)


def pick(total, wanted):
    return math.gcd(total, wanted)


def turned(modes):
    matrix = np.zeros((2 * modes, 2 * modes), np.float32)
    index = np.arange(modes)
    matrix[modes + index, index] = 1.0
    matrix[index, modes + index] = -1.0
    return matrix.astype(BF16)


def part_of(modes):
    matrix = np.zeros((2, 2 * modes, modes), np.float32)
    index = np.arange(modes)
    matrix[0, index, index] = 1.0
    matrix[1, modes + index, index] = 1.0
    return matrix.astype(BF16)


def wide(a, b):
    return jnp.dot(a, b, preferred_element_type=jnp.float32)


def line_modes(pencil, lines, turn):
    twisted = wide(pencil, turn).astype(jnp.bfloat16)
    return wide(lines, jnp.concatenate([pencil, twisted], 0))


def line_values(spectrum, lines_back, turn_back):
    twisted = wide(spectrum, turn_back).astype(jnp.bfloat16)
    return wide(lines_back, jnp.concatenate([spectrum, twisted], 0))


def whole(shape):
    return pl.BlockSpec(shape, lambda *_: (0,) * len(shape))


def mix_kernel(pencil_ref, lines_ref, turn_ref, part_ref, pack_ref, weight_ref, out_ref, coeff_ref, *, inner):
    group, outs = weight_ref.shape[1], weight_ref.shape[2]
    shape = weight_ref.shape[3:]

    @pl.when(pl.program_id(0) == 0)
    def _():
        def one_channel(i, carry):
            packed = line_modes(pencil_ref[i], lines_ref[...], turn_ref[...]).astype(jnp.bfloat16)
            coeff_ref[i, 0] = wide(packed, part_ref[0])
            coeff_ref[i, 1] = wide(packed, part_ref[1])
            return carry

        lax.fori_loop(0, group, one_channel, 0, unroll=4)

    def some_outputs(step, carry):
        first = step * inner

        def one_input(i, sums):
            real, imag = coeff_ref[i, 0], coeff_ref[i, 1]
            done = []
            for k in range(inner):
                wr = weight_ref[0, i, first + k].astype(jnp.float32)
                wi = weight_ref[1, i, first + k].astype(jnp.float32)
                done.append(sums[2 * k] + (real * wr - imag * wi))
                done.append(sums[2 * k + 1] + (real * wi + imag * wr))
            return tuple(done)

        zero = jnp.zeros(shape, jnp.float32)
        sums = lax.fori_loop(0, group, one_input, (zero,) * (2 * inner), unroll=4)
        for k in range(inner):
            out_ref[first + k] = (
                wide(sums[2 * k].astype(jnp.bfloat16), pack_ref[0])
                + wide(sums[2 * k + 1].astype(jnp.bfloat16), pack_ref[1])
            ).astype(out_ref.dtype)
        return carry

    lax.fori_loop(0, outs // inner, some_outputs, 0)


def mix(pencils, lines, turn, part, pack, weight):
    group, channels, kept, modes = weight.shape[1:]
    block = pick(channels, 8)
    return pl.pallas_call(
        functools.partial(mix_kernel, inner=pick(block, 4)),
        grid=(channels // block,),
        in_specs=[
            whole(pencils.shape), whole(lines.shape), whole(turn.shape), whole(part.shape),
            whole(pack.shape),
            pl.BlockSpec((2, group, block, kept, modes), lambda s: (0, 0, s, 0, 0)),
        ],
        out_specs=[
            pl.BlockSpec((block, kept, 2 * modes), lambda s: (s, 0, 0)),
            whole((group, 2, kept, modes)),
        ],
        out_shape=[
            jax.ShapeDtypeStruct((channels, kept, 2 * modes), jnp.bfloat16),
            jax.ShapeDtypeStruct((group, 2, kept, modes), jnp.float32),
        ],
        compiler_params=params(),
        cost_estimate=pl.CostEstimate(
            flops=4 * weight.size, bytes_accessed=4 * weight.size, transcendentals=0
        ),
        name="mix",
    )(pencils, lines, turn, part, pack, weight)


def spread_kernel(parts_ref, scale_ref, lines_ref, turn_ref, out_ref):
    def one_channel(i, carry):
        total = parts_ref[0, i].astype(jnp.float32)
        for g in range(1, parts_ref.shape[0]):
            total += parts_ref[g, i].astype(jnp.float32)
        spectrum = (total * scale_ref[...]).astype(jnp.bfloat16)
        out_ref[i] = line_values(spectrum, lines_ref[...], turn_ref[...]).astype(out_ref.dtype)
        return carry

    lax.fori_loop(0, parts_ref.shape[1], one_channel, 0, unroll=4)


def spread(parts, scale, lines, turn):
    group, width = parts.shape[1], parts.shape[3]
    shape = (group, lines.shape[0], width)
    return pl.pallas_call(
        spread_kernel,
        out_shape=jax.ShapeDtypeStruct(shape, jnp.bfloat16),
        compiler_params=params(),
        name="spread",
    )(parts, scale, lines, turn)


def gather_lines_kernel(pencil_ref, scale_ref, lines_ref, turn_ref, out_ref):
    def one_channel(i, carry):
        packed = line_modes(pencil_ref[i], lines_ref[...], turn_ref[...])
        out_ref[i] = (packed * scale_ref[...]).astype(out_ref.dtype)
        return carry

    lax.fori_loop(0, pencil_ref.shape[0], one_channel, 0, unroll=4)


def gather_lines(pencils, scale, lines, turn):
    shape = (pencils.shape[0], lines.shape[0], pencils.shape[2])
    return pl.pallas_call(
        gather_lines_kernel,
        out_shape=jax.ShapeDtypeStruct(shape, jnp.bfloat16),
        compiler_params=params(),
        name="lines",
    )(pencils, scale, lines, turn)


def adjoint_kernel(hat_ref, lines_ref, turn_ref, part_ref, pack_ref, weight_ref, out_ref, wide_ref):
    own, channels = weight_ref.shape[1], weight_ref.shape[2]
    shape = weight_ref.shape[3:]

    @pl.when(pl.program_id(0) == 0)
    def _():
        def one_channel(o, carry):
            wide_ref[o, 0] = wide(hat_ref[o], part_ref[0])
            wide_ref[o, 1] = wide(hat_ref[o], part_ref[1])
            return carry

        lax.fori_loop(0, channels, one_channel, 0, unroll=4)

    def one_output(o, sums):
        real, imag = wide_ref[o, 0], wide_ref[o, 1]
        done = []
        for k in range(own):
            wr = weight_ref[0, k, o].astype(jnp.float32)
            wi = weight_ref[1, k, o].astype(jnp.float32)
            done.append(sums[2 * k] + (real * wr + imag * wi))
            done.append(sums[2 * k + 1] + (imag * wr - real * wi))
        return tuple(done)

    zero = jnp.zeros(shape, jnp.float32)
    sums = lax.fori_loop(0, channels, one_output, (zero,) * (2 * own), unroll=4)
    for k in range(own):
        packed = wide(sums[2 * k].astype(jnp.bfloat16), pack_ref[0]) + wide(
            sums[2 * k + 1].astype(jnp.bfloat16), pack_ref[1]
        )
        values = line_values(packed.astype(jnp.bfloat16), lines_ref[...], turn_ref[...])
        out_ref[k] = values.astype(out_ref.dtype)


def adjoint_of(hat, lines, turn, part, pack, weight):
    group, channels, kept, modes = weight.shape[1:]
    block = pick(group, 2)
    length = lines.shape[0]
    return pl.pallas_call(
        adjoint_kernel,
        grid=(group // block,),
        in_specs=[
            whole(hat.shape), whole(lines.shape), whole(turn.shape), whole(part.shape),
            whole(pack.shape),
            pl.BlockSpec((2, block, channels, kept, modes), lambda s: (0, s, 0, 0, 0)),
        ],
        out_specs=[
            pl.BlockSpec((block, length, 2 * modes), lambda s: (s, 0, 0)),
            whole((channels, 2, kept, modes)),
        ],
        out_shape=[
            jax.ShapeDtypeStruct((group, length, 2 * modes), jnp.bfloat16),
            jax.ShapeDtypeStruct((channels, 2, kept, modes), jnp.float32),
        ],
        compiler_params=params(),
        cost_estimate=pl.CostEstimate(
            flops=4 * weight.size, bytes_accessed=4 * weight.size, transcendentals=0
        ),
        name="adjoint",
    )(hat, lines, turn, part, pack, weight)


def outer_kernel(coeff_ref, hat_ref, out_ref):
    own, channels = out_ref.shape[1], out_ref.shape[2]
    for i in range(own):
        cr, ci = coeff_ref[i, 0], coeff_ref[i, 1]

        def one_output(o, carry):
            hr, hi = hat_ref[o, 0], hat_ref[o, 1]
            out_ref[0, i, o] = cr * hr + ci * hi
            out_ref[1, i, o] = cr * hi - ci * hr
            return carry

        lax.fori_loop(0, channels, one_output, 0, unroll=4)


def outer(coeff, hat):
    group, _, lines, modes = coeff.shape
    channels = hat.shape[0]
    block = pick(group, 2)
    return pl.pallas_call(
        outer_kernel,
        grid=(group // block,),
        in_specs=[
            pl.BlockSpec((block, 2, lines, modes), lambda s: (s, 0, 0, 0)),
            pl.BlockSpec((channels, 2, lines, modes), lambda s: (0, 0, 0, 0)),
        ],
        out_specs=pl.BlockSpec((2, block, channels, lines, modes), lambda s: (0, s, 0, 0, 0)),
        out_shape=jax.ShapeDtypeStruct((2, group, channels, lines, modes), jnp.float32),
        compiler_params=params(),
        cost_estimate=pl.CostEstimate(
            flops=6 * group * channels * lines * modes,
            bytes_accessed=16 * group * channels * lines * modes,
            transcendentals=0,
        ),
        name="outer",
    )(coeff, hat)


ROWS_BY_ROWS = (((1,), (1,)), ((), ()))


def grid_kernel(
    modes_ref, table_ref, field_ref, cotangent_ref, point_weight_ref, repeat_ref, bias_ref,
    point_ref, hat_ref, sums_ref, total, weight_total, bias_total, mix_ref, back_ref, *, planes,
):
    step = pl.program_id(0)
    rows, channels = repeat_ref.shape

    def same_plane():
        first = lax.broadcasted_iota(jnp.int32, (rows, rows), 0) % planes
        return first == lax.broadcasted_iota(jnp.int32, (rows, rows), 1) % planes

    @pl.when(step == 0)
    def _():
        total[...] = jnp.zeros_like(total)
        weight_total[...] = jnp.zeros_like(weight_total)
        bias_total[...] = jnp.zeros_like(bias_total)
        repeat = repeat_ref[...]
        half = wide(repeat, point_weight_ref[...]).astype(jnp.bfloat16)
        full = lax.dot_general(half, repeat, ROWS_BY_ROWS, preferred_element_type=jnp.float32)
        back = jnp.where(same_plane(), full, 0.0)
        back_ref[...] = back.astype(jnp.bfloat16)
        mix_ref[...] = back.T.astype(jnp.bfloat16)

    table = table_ref[...]
    field = field_ref[...]
    pre_act = lax.dot_general(
        modes_ref[...], table, ROWS_BY_ROWS, preferred_element_type=jnp.float32
    )
    pre_act += jnp.dot(mix_ref[...], field, preferred_element_type=jnp.float32)
    pre_act += bias_ref[...]
    grad_wide = cotangent_ref[...].astype(jnp.float32) * gelu_grad(pre_act)
    grad_pre = grad_wide.astype(jnp.bfloat16)
    point_ref[...] = jnp.dot(
        back_ref[...], grad_pre, preferred_element_type=jnp.float32
    ).astype(point_ref.dtype)
    total[...] += jnp.dot(grad_pre, table, preferred_element_type=jnp.float32)
    weight_total[...] += lax.dot_general(
        field, grad_pre, ROWS_BY_ROWS, preferred_element_type=jnp.float32
    )
    bias_total[...] += jnp.sum(grad_pre.astype(jnp.float32), axis=1, keepdims=True)

    @pl.when(step == pl.num_programs(0) - 1)
    def _():
        width = hat_ref.shape[-1]
        for s in range(hat_ref.shape[0]):
            hat_ref[s] = total[:, s * width : (s + 1) * width].astype(hat_ref.dtype)
        repeat = repeat_ref[...].astype(jnp.float32)
        kept = jnp.where(same_plane(), weight_total[...], 0.0)
        columns = jnp.dot(
            kept, repeat, precision=lax.Precision.HIGHEST, preferred_element_type=jnp.float32
        )
        both = (((0,), (0,)), ((), ()))
        sums_ref[:channels] = lax.dot_general(
            repeat, columns, both, precision=lax.Precision.HIGHEST,
            preferred_element_type=jnp.float32,
        )
        spread_bias = jnp.broadcast_to(bias_total[...], (rows, 8))
        sums_ref[channels:] = lax.dot_general(
            spread_bias, repeat, both, precision=lax.Precision.HIGHEST,
            preferred_element_type=jnp.float32,
        )


def grid_stage(modes, table, field, cotangent, point_weight, bias, planes, parts):
    rows, width = modes.shape
    cells = table.shape[0]
    channels = point_weight.shape[0]
    block = pick(cells, 512)
    along = lambda s: (0, s)
    repeat = jnp.asarray(np.repeat(np.eye(channels, dtype=np.float32), planes, 0).astype(BF16))
    return pl.pallas_call(
        functools.partial(grid_kernel, planes=planes),
        grid=(cells // block,),
        in_specs=[
            whole((rows, width)),
            pl.BlockSpec((block, width), lambda s: (s, 0)),
            pl.BlockSpec((rows, block), along),
            pl.BlockSpec((rows, block), along),
            whole((channels, channels)),
            whole((rows, channels)),
            whole((rows, 1)),
        ],
        out_specs=[
            pl.BlockSpec((rows, block), along),
            whole((parts, rows, width // parts)),
            whole((channels + 8, channels)),
        ],
        out_shape=[
            jax.ShapeDtypeStruct((rows, cells), jnp.bfloat16),
            jax.ShapeDtypeStruct((parts, rows, width // parts), jnp.bfloat16),
            jax.ShapeDtypeStruct((channels + 8, channels), jnp.float32),
        ],
        scratch_shapes=[
            pltpu.VMEM((rows, width), jnp.float32),
            pltpu.VMEM((rows, rows), jnp.float32),
            pltpu.VMEM((rows, 1), jnp.float32),
            pltpu.VMEM((rows, rows), jnp.bfloat16),
            pltpu.VMEM((rows, rows), jnp.bfloat16),
        ],
        compiler_params=params(),
        cost_estimate=pl.CostEstimate(
            flops=2 * rows * cells * (2 * width + 3 * rows),
            bytes_accessed=2 * cells * (width + 3 * rows),
            transcendentals=2 * rows * cells,
        ),
        name="grid",
    )(modes, table, field, cotangent, point_weight, repeat, bias)


def finish_kernel(modes_ref, table_ref, point_ref, out_ref):
    back = lax.dot_general(
        modes_ref[...], table_ref[...], ROWS_BY_ROWS, preferred_element_type=jnp.float32
    )
    point = jnp.swapaxes(point_ref[...].astype(jnp.float32), 0, 1)
    out_ref[...] = (back + point.reshape(back.shape)).astype(out_ref.dtype)


def finish(modes, table, point):
    chans, group, planes, cells = point.shape
    rows, width = modes.shape
    block = pick(cells, 512)
    return pl.pallas_call(
        finish_kernel,
        grid=(cells // block,),
        in_specs=[
            whole((rows, width)),
            pl.BlockSpec((block, width), lambda s: (s, 0)),
            pl.BlockSpec((chans, group, planes, block), lambda s: (0, 0, 0, s)),
        ],
        out_specs=pl.BlockSpec((rows, block), lambda s: (0, s)),
        out_shape=jax.ShapeDtypeStruct((rows, cells), jnp.bfloat16),
        compiler_params=params(),
        cost_estimate=pl.CostEstimate(
            flops=2 * rows * cells * width,
            bytes_accessed=2 * cells * (width + 2 * rows),
            transcendentals=0,
        ),
        name="finish",
    )(modes, table, point)


def begin_kernel(chan_ref, field_ref, table_ref, out_ref, total):
    step = pl.program_id(0)
    field = field_ref[...].reshape(total.shape[0], field_ref.shape[2])
    part = wide(field, table_ref[...])

    @pl.when(step == 0)
    def _():
        total[...] = part

    @pl.when(step > 0)
    def _():
        total[...] += part

    @pl.when(step == pl.num_programs(0) - 1)
    def _():
        width = out_ref.shape[-1]
        for s in range(out_ref.shape[0]):
            out_ref[s] = total[:, s * width : (s + 1) * width].astype(out_ref.dtype)


def begin(chan_index, field, table, group, parts):
    planes, cells = field.shape[1:]
    width = table.shape[1]
    rows = group * planes
    block = pick(cells, 1024)
    return pl.pallas_call(
        begin_kernel,
        grid_spec=pltpu.PrefetchScalarGridSpec(
            num_scalar_prefetch=1,
            grid=(cells // block,),
            in_specs=[
                pl.BlockSpec((group, planes, block), lambda s, chan: (chan[0], 0, s)),
                pl.BlockSpec((block, width), lambda s, chan: (s, 0)),
            ],
            out_specs=whole((parts, rows, width // parts)),
            scratch_shapes=[pltpu.VMEM((rows, width), jnp.float32)],
        ),
        out_shape=jax.ShapeDtypeStruct((parts, rows, width // parts), jnp.bfloat16),
        compiler_params=params(),
        cost_estimate=pl.CostEstimate(
            flops=2 * rows * cells * width,
            bytes_accessed=2 * cells * (width + rows),
            transcendentals=0,
        ),
        name="begin",
    )(chan_index.reshape(1), field, table)


def exchange_kernel(axes, sizes, blocks, *refs):
    count = len(blocks)
    ins, outs = refs[:count], refs[count : 2 * count]
    send, recv, local = refs[2 * count :]
    total = math.prod(sizes)
    last = sizes[-1]
    me = lax.axis_index(axes[0])
    if len(axes) == 2:
        me = me * last + lax.axis_index(axes[1])

    def place(index):
        if len(axes) == 2:
            return {axes[0]: lax.div(index, last), axes[1]: lax.rem(index, last)}
        return {axes[0]: index}

    def source(a, index):
        if blocks[a] == total:
            return ins[a].at[index]
        if blocks[a] == 1:
            return ins[a].at[0]
        return ins[a].at[lax.rem(index, last)]

    def copy(a, shift):
        peer = lax.rem(me + shift, total)
        return pltpu.make_async_remote_copy(
            src_ref=source(a, peer),
            dst_ref=outs[a].at[me],
            send_sem=send.at[a, shift],
            recv_sem=recv.at[a, shift],
            device_id=place(peer),
            device_id_type=pl.DeviceIdType.MESH,
        )

    barrier = pltpu.get_barrier_semaphore()

    def greet(shift, carry):
        pl.semaphore_signal(
            barrier, inc=1, device_id=place(lax.rem(me + shift, total)),
            device_id_type=pl.DeviceIdType.MESH,
        )
        return carry

    def start(shift, carry):
        for a in range(count):
            copy(a, shift).start()
        return carry

    def wait(shift, carry):
        for a in range(count):
            copy(a, shift).wait()
        return carry

    lax.fori_loop(1, total, greet, 0)
    own = [
        pltpu.make_async_copy(source(a, me), outs[a].at[me], local.at[a]) for a in range(count)
    ]
    for one in own:
        one.start()
    pl.semaphore_wait(barrier, total - 1)
    lax.fori_loop(1, total, start, 0)
    for one in own:
        one.wait()
    lax.fori_loop(1, total, wait, 0)


def exchange(arrays, axes, sizes, collective_id):
    total = math.prod(sizes)
    blocks = tuple(array.shape[0] for array in arrays)
    anywhere = pl.BlockSpec(memory_space=pl.ANY)
    return pl.pallas_call(
        functools.partial(exchange_kernel, axes, sizes, blocks),
        in_specs=[anywhere] * len(arrays),
        out_specs=[anywhere] * len(arrays),
        out_shape=[
            jax.ShapeDtypeStruct((total,) + array.shape[1:], array.dtype) for array in arrays
        ],
        scratch_shapes=[
            pltpu.SemaphoreType.DMA((len(arrays), total)),
            pltpu.SemaphoreType.DMA((len(arrays), total)),
            pltpu.SemaphoreType.DMA((len(arrays),)),
        ],
        compiler_params=pltpu.CompilerParams(
            collective_id=collective_id, has_side_effects=True, vmem_limit_bytes=VMEM_LIMIT
        ),
        cost_estimate=pl.CostEstimate(
            flops=0, bytes_accessed=sum(8 * 2 * a.size for a in arrays), transcendentals=0
        ),
        name="exchange",
    )(*arrays)


def pad_planes(array, dim, spare):
    if not spare:
        return array
    return jnp.pad(array, [(0, spare if d == dim else 0) for d in range(array.ndim)])


def body(slabs, chans, field, cotangent, spectral_weight, point_weight, point_bias):
    channels, planes, cells = field.shape
    group = spectral_weight.shape[1]
    modes = spectral_weight.shape[3]
    own_planes = -(-planes // chans)
    spare = own_planes * chans - planes
    length = planes * slabs
    width = 2 * modes
    tiled = planes % 16 == 0 and own_planes % 8 == 0 and width % 128 == 0
    everyone = ("slab", "chan"), (slabs, chans)
    table = lax.optimization_barrier(jnp.asarray(plane_table(slabs)))
    cosine, sine = line_tables(length)
    lines = jnp.asarray(np.concatenate([cosine, sine], 1))
    lines_back = jnp.asarray(np.concatenate([cosine.T, sine.T], 1))
    turn, turn_back = jnp.asarray(turned(modes)), jnp.asarray(turned(modes).T)
    part, pack = jnp.asarray(part_of(modes)), jnp.asarray(np.swapaxes(part_of(modes), 1, 2))
    slab_index = lax.axis_index("slab")
    chan_index = lax.axis_index("chan")
    weight = jnp.swapaxes(spectral_weight, 3, 4)
    mode_index = slab_index * modes + jnp.arange(width, dtype=jnp.int32) % modes
    scale = (jnp.where(mode_index // MY == 0, 1.0, 2.0) / (length * cells)).astype(jnp.float32)
    scale = scale[None]

    if tiled:
        sections = begin(chan_index, field, table, group, slabs)
    else:
        own_field = lax.dynamic_slice_in_dim(field, chan_index * group, group, 0)
        sections = wide(own_field.reshape(group * planes, cells), table).astype(jnp.bfloat16)
        sections = jnp.moveaxis(sections.reshape(group * planes, slabs, width), 1, 0)
    (pencils,) = exchange([sections], ("slab",), (slabs,), 0)
    pencils = jnp.moveaxis(pencils.reshape(slabs, group, planes, width), 1, 0)
    partial, coeff = mix(
        pencils.reshape(group, length, width), lines, turn, part, pack, weight
    )
    (parts,) = exchange([partial.reshape(chans, group, MX, width)], ("chan",), (chans,), 1)
    pencils = spread(parts, scale, lines_back, turn_back)
    pencils = pad_planes(pencils.reshape(group, slabs, planes, width), 2, spare)
    pencils = pencils.reshape(group, slabs, chans, own_planes, width)
    pencils = jnp.transpose(pencils, (1, 2, 0, 3, 4))
    pencils = pencils.reshape(slabs * chans, group, own_planes, width)
    slabs_in = lax.all_to_all(
        pencils, ("slab", "chan"), split_axis=0, concat_axis=0, tiled=True
    )
    slabs_in = slabs_in.reshape(slabs, channels, own_planes, width)
    rows = channels * own_planes
    slabs_in = jnp.transpose(slabs_in, (1, 2, 0, 3)).reshape(rows, slabs * width)

    first_plane = chan_index * own_planes
    plane_field = lax.dynamic_slice_in_dim(
        pad_planes(field, 1, spare), first_plane, own_planes, 1
    )
    plane_cotangent = lax.dynamic_slice_in_dim(
        pad_planes(cotangent, 1, spare), first_plane, own_planes, 1
    )
    point, hat_rows, sums = grid_stage(
        slabs_in,
        table,
        plane_field.reshape(rows, cells),
        plane_cotangent.reshape(rows, cells),
        point_weight,
        jnp.repeat(point_bias.astype(jnp.float32), own_planes)[:, None],
        own_planes,
        slabs if tiled else 1,
    )
    point = lax.all_to_all(
        point.reshape(chans, group, own_planes, cells),
        "chan", split_axis=0, concat_axis=0, tiled=True,
    )
    if not tiled:
        hat_rows = jnp.moveaxis(hat_rows.reshape(rows, slabs, width), 1, 0)
    hat_rows = hat_rows.reshape(slabs * chans, group, own_planes, width)
    own_sums = sums[:channels].reshape(chans, group, channels)
    bias_sums = jnp.broadcast_to(sums[channels:][None], (chans, 8, channels))
    own_sums = jnp.concatenate([own_sums, bias_sums], 1)
    pencils, all_sums = exchange([hat_rows, own_sums], *everyone, 2)
    pencils = jnp.moveaxis(pencils.reshape(slabs, chans, group, own_planes, width), 2, 0)
    pencils = pencils.reshape(group, slabs, chans * own_planes, width)[:, :, :planes]
    part_hat = gather_lines(pencils.reshape(group, length, width), scale, lines, turn)
    (hat,) = exchange([part_hat[None]], ("chan",), (chans,), 3)

    pencils, hat = adjoint_of(
        hat.reshape(channels, MX, width), lines_back, turn_back, part, pack, weight
    )
    pencils = pencils.reshape(group, slabs, planes, width)
    pencils = lax.all_to_all(
        jnp.moveaxis(pencils, 1, 0), "slab", split_axis=0, concat_axis=0, tiled=True
    )
    grad_spectral = jnp.swapaxes(outer(coeff, hat), 3, 4)
    pencils = jnp.moveaxis(pencils, 0, 2).reshape(group * planes, slabs * width)
    if tiled:
        grad_input = finish(pencils, table, point).reshape(group, planes, cells)
    else:
        back = lax.dot_general(pencils, table, ROWS_BY_ROWS, preferred_element_type=jnp.float32)
        back = back.reshape(group, planes, cells)
        point = jnp.moveaxis(point, 0, 1).reshape(group, chans * own_planes, cells)[:, :planes]
        grad_input = (back + point.astype(jnp.float32)).astype(jnp.bfloat16)

    sums = jnp.sum(all_sums, 0) * (1.0 / math.sqrt(length * cells))
    return (grad_input, grad_spectral, sums[:group], sums[group])


def solution(mesh):
    placed = (
        P(None, "slab", None),
        P(None, "slab", None),
        P(None, "chan", None, "slab", None),
        P(),
        P(),
    )
    return jax.shard_map(
        functools.partial(body, mesh.shape["slab"], mesh.shape["chan"]),
        mesh=mesh,
        in_specs=placed,
        out_specs=(
            P("chan", "slab", None),
            P(None, "chan", None, "slab", None),
            P("chan", None),
            P(),
        ),
        check_vma=False,
    )
```

```python
import functools
import math

import jax
import jax.numpy as jnp
import ml_dtypes
import numpy as np
from jax import lax
from jax.experimental import pallas as pl
from jax.experimental.pallas import tpu as pltpu
from jax.sharding import PartitionSpec as P

MX = 32
MY = 32
MZ = 16
NY = 64
NZ = 64

BF16 = ml_dtypes.bfloat16
VMEM_LIMIT = 50 * 1024 * 1024


def kept_modes(total, length):
    mode_index = np.arange(total, dtype=np.int32)
    return np.where(mode_index < total // 2, mode_index, mode_index - total + length)


def rounded_waves(frequency, length):
    positions = np.arange(length, dtype=np.int32)
    wound_up = frequency[:, None] * positions[None, :] % length
    angle = np.float32(2.0 * math.pi / length) * wound_up.astype(np.float32)
    cosine = np.cos(angle).astype(BF16).astype(np.float32)
    sine = np.sin(angle).astype(BF16).astype(np.float32)
    return cosine, sine


def plane_table(slabs):
    cosine_z, sine_z = rounded_waves(np.arange(MZ, dtype=np.int32), NZ)
    cosine_y, sine_y = rounded_waves(kept_modes(MY, NY), NY)
    cz, sz = cosine_z.T[None, :, :, None], sine_z.T[None, :, :, None]
    cy, sy = cosine_y.T[:, None, None, :], sine_y.T[:, None, None, :]
    real = (cz * cy - sz * sy).reshape(NY * NZ, slabs, 1, -1)
    imag = -(cz * sy + sz * cy).reshape(NY * NZ, slabs, 1, -1)
    return np.concatenate([real, imag], 2).reshape(NY * NZ, -1).astype(BF16)


def line_tables(length):
    cosine, sine = rounded_waves(kept_modes(MX, length), length)
    return cosine.astype(BF16), sine.astype(BF16)


def gelu_grad(pre_act):
    normal_cdf = 0.5 * (1.0 + lax.erf(pre_act * (1.0 / math.sqrt(2.0))))
    normal_pdf = jnp.exp(-0.5 * pre_act * pre_act) * (1.0 / math.sqrt(2.0 * math.pi))
    return normal_cdf + pre_act * normal_pdf


def params():
    return pltpu.CompilerParams(vmem_limit_bytes=VMEM_LIMIT)


def pick(total, wanted):
    return math.gcd(total, wanted)


def turned(modes):
    matrix = np.zeros((2 * modes, 2 * modes), np.float32)
    index = np.arange(modes)
    matrix[modes + index, index] = 1.0
    matrix[index, modes + index] = -1.0
    return matrix.astype(BF16)


def part_of(modes):
    matrix = np.zeros((2, 2 * modes, modes), np.float32)
    index = np.arange(modes)
    matrix[0, index, index] = 1.0
    matrix[1, modes + index, index] = 1.0
    return matrix.astype(BF16)


def wide(a, b):
    return jnp.dot(a, b, preferred_element_type=jnp.float32)


def line_modes(pencil, lines, turn):
    twisted = wide(pencil, turn).astype(jnp.bfloat16)
    return wide(lines, jnp.concatenate([pencil, twisted], 0))


def line_values(spectrum, lines_back, turn_back):
    twisted = wide(spectrum, turn_back).astype(jnp.bfloat16)
    return wide(lines_back, jnp.concatenate([spectrum, twisted], 0))


def whole(shape):
    return pl.BlockSpec(shape, lambda *_: (0,) * len(shape))


def mix_kernel(pencil_ref, lines_ref, turn_ref, part_ref, pack_ref, weight_ref, out_ref, coeff_ref, *, inner):
    group, outs = weight_ref.shape[1], weight_ref.shape[2]
    shape = weight_ref.shape[3:]

    @pl.when(pl.program_id(0) == 0)
    def _():
        def one_channel(i, carry):
            packed = line_modes(pencil_ref[i], lines_ref[...], turn_ref[...]).astype(jnp.bfloat16)
            coeff_ref[i, 0] = wide(packed, part_ref[0])
            coeff_ref[i, 1] = wide(packed, part_ref[1])
            return carry

        lax.fori_loop(0, group, one_channel, 0, unroll=4)

    def some_outputs(step, carry):
        first = step * inner

        def one_input(i, sums):
            real, imag = coeff_ref[i, 0], coeff_ref[i, 1]
            done = []
            for k in range(inner):
                wr = weight_ref[0, i, first + k].astype(jnp.float32)
                wi = weight_ref[1, i, first + k].astype(jnp.float32)
                done.append(sums[2 * k] + (real * wr - imag * wi))
                done.append(sums[2 * k + 1] + (real * wi + imag * wr))
            return tuple(done)

        zero = jnp.zeros(shape, jnp.float32)
        sums = lax.fori_loop(0, group, one_input, (zero,) * (2 * inner), unroll=4)
        for k in range(inner):
            out_ref[first + k] = (
                wide(sums[2 * k].astype(jnp.bfloat16), pack_ref[0])
                + wide(sums[2 * k + 1].astype(jnp.bfloat16), pack_ref[1])
            ).astype(out_ref.dtype)
        return carry

    lax.fori_loop(0, outs // inner, some_outputs, 0)


def mix(pencils, lines, turn, part, pack, weight):
    group, channels, kept, modes = weight.shape[1:]
    block = pick(channels, 8)
    return pl.pallas_call(
        functools.partial(mix_kernel, inner=pick(block, 4)),
        grid=(channels // block,),
        in_specs=[
            whole(pencils.shape), whole(lines.shape), whole(turn.shape), whole(part.shape),
            whole(pack.shape),
            pl.BlockSpec((2, group, block, kept, modes), lambda s: (0, 0, s, 0, 0)),
        ],
        out_specs=[
            pl.BlockSpec((block, kept, 2 * modes), lambda s: (s, 0, 0)),
            whole((group, 2, kept, modes)),
        ],
        out_shape=[
            jax.ShapeDtypeStruct((channels, kept, 2 * modes), jnp.bfloat16),
            jax.ShapeDtypeStruct((group, 2, kept, modes), jnp.float32),
        ],
        compiler_params=params(),
        cost_estimate=pl.CostEstimate(
            flops=4 * weight.size, bytes_accessed=4 * weight.size, transcendentals=0
        ),
        name="mix",
    )(pencils, lines, turn, part, pack, weight)


def spread_kernel(parts_ref, scale_ref, lines_ref, turn_ref, out_ref):
    def one_channel(i, carry):
        total = parts_ref[0, i].astype(jnp.float32)
        for g in range(1, parts_ref.shape[0]):
            total += parts_ref[g, i].astype(jnp.float32)
        spectrum = (total * scale_ref[...]).astype(jnp.bfloat16)
        out_ref[i] = line_values(spectrum, lines_ref[...], turn_ref[...]).astype(out_ref.dtype)
        return carry

    lax.fori_loop(0, parts_ref.shape[1], one_channel, 0, unroll=4)


def spread(parts, scale, lines, turn):
    group, width = parts.shape[1], parts.shape[3]
    shape = (group, lines.shape[0], width)
    return pl.pallas_call(
        spread_kernel,
        out_shape=jax.ShapeDtypeStruct(shape, jnp.bfloat16),
        compiler_params=params(),
        name="spread",
    )(parts, scale, lines, turn)


def gather_lines_kernel(pencil_ref, scale_ref, lines_ref, turn_ref, out_ref):
    def one_channel(i, carry):
        packed = line_modes(pencil_ref[i], lines_ref[...], turn_ref[...])
        out_ref[i] = (packed * scale_ref[...]).astype(out_ref.dtype)
        return carry

    lax.fori_loop(0, pencil_ref.shape[0], one_channel, 0, unroll=4)


def gather_lines(pencils, scale, lines, turn):
    shape = (pencils.shape[0], lines.shape[0], pencils.shape[2])
    return pl.pallas_call(
        gather_lines_kernel,
        out_shape=jax.ShapeDtypeStruct(shape, jnp.bfloat16),
        compiler_params=params(),
        name="lines",
    )(pencils, scale, lines, turn)


def adjoint_kernel(hat_ref, lines_ref, turn_ref, part_ref, pack_ref, weight_ref, out_ref, wide_ref):
    own, channels = weight_ref.shape[1], weight_ref.shape[2]
    shape = weight_ref.shape[3:]

    @pl.when(pl.program_id(0) == 0)
    def _():
        def one_channel(o, carry):
            wide_ref[o, 0] = wide(hat_ref[o], part_ref[0])
            wide_ref[o, 1] = wide(hat_ref[o], part_ref[1])
            return carry

        lax.fori_loop(0, channels, one_channel, 0, unroll=4)

    def one_output(o, sums):
        real, imag = wide_ref[o, 0], wide_ref[o, 1]
        done = []
        for k in range(own):
            wr = weight_ref[0, k, o].astype(jnp.float32)
            wi = weight_ref[1, k, o].astype(jnp.float32)
            done.append(sums[2 * k] + (real * wr + imag * wi))
            done.append(sums[2 * k + 1] + (imag * wr - real * wi))
        return tuple(done)

    zero = jnp.zeros(shape, jnp.float32)
    sums = lax.fori_loop(0, channels, one_output, (zero,) * (2 * own), unroll=4)
    for k in range(own):
        packed = wide(sums[2 * k].astype(jnp.bfloat16), pack_ref[0]) + wide(
            sums[2 * k + 1].astype(jnp.bfloat16), pack_ref[1]
        )
        values = line_values(packed.astype(jnp.bfloat16), lines_ref[...], turn_ref[...])
        out_ref[k] = values.astype(out_ref.dtype)


def adjoint_of(hat, lines, turn, part, pack, weight):
    group, channels, kept, modes = weight.shape[1:]
    block = pick(group, 2)
    length = lines.shape[0]
    return pl.pallas_call(
        adjoint_kernel,
        grid=(group // block,),
        in_specs=[
            whole(hat.shape), whole(lines.shape), whole(turn.shape), whole(part.shape),
            whole(pack.shape),
            pl.BlockSpec((2, block, channels, kept, modes), lambda s: (0, s, 0, 0, 0)),
        ],
        out_specs=[
            pl.BlockSpec((block, length, 2 * modes), lambda s: (s, 0, 0)),
            whole((channels, 2, kept, modes)),
        ],
        out_shape=[
            jax.ShapeDtypeStruct((group, length, 2 * modes), jnp.bfloat16),
            jax.ShapeDtypeStruct((channels, 2, kept, modes), jnp.float32),
        ],
        compiler_params=params(),
        cost_estimate=pl.CostEstimate(
            flops=4 * weight.size, bytes_accessed=4 * weight.size, transcendentals=0
        ),
        name="adjoint",
    )(hat, lines, turn, part, pack, weight)


def outer_kernel(coeff_ref, hat_ref, out_ref):
    own, channels = out_ref.shape[1], out_ref.shape[2]
    for i in range(own):
        cr, ci = coeff_ref[i, 0], coeff_ref[i, 1]

        def one_output(o, carry):
            hr, hi = hat_ref[o, 0], hat_ref[o, 1]
            out_ref[0, i, o] = cr * hr + ci * hi
            out_ref[1, i, o] = cr * hi - ci * hr
            return carry

        lax.fori_loop(0, channels, one_output, 0, unroll=4)


def outer(coeff, hat):
    group, _, lines, modes = coeff.shape
    channels = hat.shape[0]
    block = pick(group, 2)
    return pl.pallas_call(
        outer_kernel,
        grid=(group // block,),
        in_specs=[
            pl.BlockSpec((block, 2, lines, modes), lambda s: (s, 0, 0, 0)),
            pl.BlockSpec((channels, 2, lines, modes), lambda s: (0, 0, 0, 0)),
        ],
        out_specs=pl.BlockSpec((2, block, channels, lines, modes), lambda s: (0, s, 0, 0, 0)),
        out_shape=jax.ShapeDtypeStruct((2, group, channels, lines, modes), jnp.float32),
        compiler_params=params(),
        cost_estimate=pl.CostEstimate(
            flops=6 * group * channels * lines * modes,
            bytes_accessed=16 * group * channels * lines * modes,
            transcendentals=0,
        ),
        name="outer",
    )(coeff, hat)


ROWS_BY_ROWS = (((1,), (1,)), ((), ()))


def grid_kernel(
    chan_ref, modes_ref, table_ref, field_ref, cotangent_ref, point_weight_ref, repeat_ref, bias_ref,
    point_ref, hat_ref, sums_ref, total, weight_total, bias_total, mix_ref, back_ref, *, planes,
):
    step = pl.program_id(0)
    rows, channels = repeat_ref.shape

    def same_plane():
        first = lax.broadcasted_iota(jnp.int32, (rows, rows), 0) % planes
        return first == lax.broadcasted_iota(jnp.int32, (rows, rows), 1) % planes

    @pl.when(step == 0)
    def _():
        total[...] = jnp.zeros_like(total)
        weight_total[...] = jnp.zeros_like(weight_total)
        bias_total[...] = jnp.zeros_like(bias_total)
        repeat = repeat_ref[...]
        half = wide(repeat, point_weight_ref[...]).astype(jnp.bfloat16)
        full = lax.dot_general(half, repeat, ROWS_BY_ROWS, preferred_element_type=jnp.float32)
        back = jnp.where(same_plane(), full, 0.0)
        back_ref[...] = back.astype(jnp.bfloat16)
        mix_ref[...] = back.T.astype(jnp.bfloat16)

    table = table_ref[...]
    shape = (rows, field_ref.shape[-1])
    field = field_ref[...].astype(jnp.float32).reshape(shape).astype(jnp.bfloat16)
    pre_act = lax.dot_general(
        modes_ref[...], table, ROWS_BY_ROWS, preferred_element_type=jnp.float32
    )
    pre_act += jnp.dot(mix_ref[...], field, preferred_element_type=jnp.float32)
    pre_act += bias_ref[...]
    grad_wide = cotangent_ref[...].astype(jnp.float32).reshape(shape) * gelu_grad(pre_act)
    grad_pre = grad_wide.astype(jnp.bfloat16)
    point_ref[...] = jnp.dot(
        back_ref[...], grad_pre, preferred_element_type=jnp.float32
    ).astype(point_ref.dtype)
    total[...] += jnp.dot(grad_pre, table, preferred_element_type=jnp.float32)
    weight_total[...] += lax.dot_general(
        field, grad_pre, ROWS_BY_ROWS, preferred_element_type=jnp.float32
    )
    bias_total[...] += jnp.sum(grad_pre.astype(jnp.float32), axis=1, keepdims=True)

    @pl.when(step == pl.num_programs(0) - 1)
    def _():
        width = hat_ref.shape[-1]
        for s in range(hat_ref.shape[0]):
            hat_ref[s] = total[:, s * width : (s + 1) * width].astype(hat_ref.dtype)
        repeat = repeat_ref[...].astype(jnp.float32)
        kept = jnp.where(same_plane(), weight_total[...], 0.0)
        columns = jnp.dot(
            kept, repeat, precision=lax.Precision.HIGHEST, preferred_element_type=jnp.float32
        )
        both = (((0,), (0,)), ((), ()))
        sums_ref[:channels] = lax.dot_general(
            repeat, columns, both, precision=lax.Precision.HIGHEST,
            preferred_element_type=jnp.float32,
        )
        spread_bias = jnp.broadcast_to(bias_total[...], (rows, 8))
        sums_ref[channels:] = lax.dot_general(
            spread_bias, repeat, both, precision=lax.Precision.HIGHEST,
            preferred_element_type=jnp.float32,
        )


def grid_stage(chan_index, modes, table, field, cotangent, point_weight, bias, parts):
    rows, width = modes.shape
    cells = table.shape[0]
    channels = point_weight.shape[0]
    planes = rows // channels
    block = pick(cells, 512)
    repeat = jnp.asarray(np.repeat(np.eye(channels, dtype=np.float32), planes, 0).astype(BF16))
    own = pl.BlockSpec((channels, planes, block), lambda s, chan: (0, chan[0], s))
    return pl.pallas_call(
        functools.partial(grid_kernel, planes=planes),
        grid_spec=pltpu.PrefetchScalarGridSpec(
            num_scalar_prefetch=1,
            grid=(cells // block,),
            in_specs=[
                whole((rows, width)),
                pl.BlockSpec((block, width), lambda s, chan: (s, 0)),
                own,
                own,
                whole((channels, channels)),
                whole((rows, channels)),
                whole((rows, 1)),
            ],
            out_specs=[
                pl.BlockSpec((rows, block), lambda s, chan: (0, s)),
                whole((parts, rows, width // parts)),
                whole((channels + 8, channels)),
            ],
            scratch_shapes=[
                pltpu.VMEM((rows, width), jnp.float32),
                pltpu.VMEM((rows, rows), jnp.float32),
                pltpu.VMEM((rows, 1), jnp.float32),
                pltpu.VMEM((rows, rows), jnp.bfloat16),
                pltpu.VMEM((rows, rows), jnp.bfloat16),
            ],
        ),
        out_shape=[
            jax.ShapeDtypeStruct((rows, cells), jnp.bfloat16),
            jax.ShapeDtypeStruct((parts, rows, width // parts), jnp.bfloat16),
            jax.ShapeDtypeStruct((channels + 8, channels), jnp.float32),
        ],
        compiler_params=params(),
        cost_estimate=pl.CostEstimate(
            flops=2 * rows * cells * (2 * width + 3 * rows),
            bytes_accessed=2 * cells * (width + 3 * rows),
            transcendentals=2 * rows * cells,
        ),
        name="grid",
    )(chan_index.reshape(1), modes, table, field, cotangent, point_weight, repeat, bias)


def finish_kernel(modes_ref, table_ref, point_ref, out_ref):
    back = lax.dot_general(
        modes_ref[...], table_ref[...], ROWS_BY_ROWS, preferred_element_type=jnp.float32
    )
    point = jnp.swapaxes(point_ref[...].astype(jnp.float32), 0, 1)
    out_ref[...] = (back + point.reshape(back.shape)).astype(out_ref.dtype)


def finish(modes, table, point):
    chans, group, planes, cells = point.shape
    rows, width = modes.shape
    block = pick(cells, 512)
    return pl.pallas_call(
        finish_kernel,
        grid=(cells // block,),
        in_specs=[
            whole((rows, width)),
            pl.BlockSpec((block, width), lambda s: (s, 0)),
            pl.BlockSpec((chans, group, planes, block), lambda s: (0, 0, 0, s)),
        ],
        out_specs=pl.BlockSpec((rows, block), lambda s: (0, s)),
        out_shape=jax.ShapeDtypeStruct((rows, cells), jnp.bfloat16),
        compiler_params=params(),
        cost_estimate=pl.CostEstimate(
            flops=2 * rows * cells * width,
            bytes_accessed=2 * cells * (width + 2 * rows),
            transcendentals=0,
        ),
        name="finish",
    )(modes, table, point)


def begin_kernel(chan_ref, field_ref, table_ref, out_ref, total):
    step = pl.program_id(0)
    field = field_ref[...].reshape(total.shape[0], field_ref.shape[2])
    part = wide(field, table_ref[...])

    @pl.when(step == 0)
    def _():
        total[...] = part

    @pl.when(step > 0)
    def _():
        total[...] += part

    @pl.when(step == pl.num_programs(0) - 1)
    def _():
        width = out_ref.shape[-1]
        for s in range(out_ref.shape[0]):
            out_ref[s] = total[:, s * width : (s + 1) * width].astype(out_ref.dtype)


def begin(chan_index, field, table, group, parts):
    planes, cells = field.shape[1:]
    width = table.shape[1]
    rows = group * planes
    block = pick(cells, 1024)
    return pl.pallas_call(
        begin_kernel,
        grid_spec=pltpu.PrefetchScalarGridSpec(
            num_scalar_prefetch=1,
            grid=(cells // block,),
            in_specs=[
                pl.BlockSpec((group, planes, block), lambda s, chan: (chan[0], 0, s)),
                pl.BlockSpec((block, width), lambda s, chan: (s, 0)),
            ],
            out_specs=whole((parts, rows, width // parts)),
            scratch_shapes=[pltpu.VMEM((rows, width), jnp.float32)],
        ),
        out_shape=jax.ShapeDtypeStruct((parts, rows, width // parts), jnp.bfloat16),
        compiler_params=params(),
        cost_estimate=pl.CostEstimate(
            flops=2 * rows * cells * width,
            bytes_accessed=2 * cells * (width + rows),
            transcendentals=0,
        ),
        name="begin",
    )(chan_index.reshape(1), field, table)


def exchange_kernel(axes, sizes, blocks, *refs):
    count = len(blocks)
    ins, outs = refs[:count], refs[count : 2 * count]
    send, recv, local = refs[2 * count :]
    total = math.prod(sizes)
    last = sizes[-1]
    me = lax.axis_index(axes[0])
    if len(axes) == 2:
        me = me * last + lax.axis_index(axes[1])

    def place(index):
        if len(axes) == 2:
            return {axes[0]: lax.div(index, last), axes[1]: lax.rem(index, last)}
        return {axes[0]: index}

    def source(a, index):
        if blocks[a] == total:
            return ins[a].at[index]
        if blocks[a] == 1:
            return ins[a].at[0]
        return ins[a].at[lax.rem(index, last)]

    def copy(a, shift):
        peer = lax.rem(me + shift, total)
        return pltpu.make_async_remote_copy(
            src_ref=source(a, peer),
            dst_ref=outs[a].at[me],
            send_sem=send.at[a, shift],
            recv_sem=recv.at[a, shift],
            device_id=place(peer),
            device_id_type=pl.DeviceIdType.MESH,
        )

    barrier = pltpu.get_barrier_semaphore()

    def greet(shift, carry):
        pl.semaphore_signal(
            barrier, inc=1, device_id=place(lax.rem(me + shift, total)),
            device_id_type=pl.DeviceIdType.MESH,
        )
        return carry

    def start(shift, carry):
        for a in range(count):
            copy(a, shift).start()
        return carry

    def wait(shift, carry):
        for a in range(count):
            copy(a, shift).wait()
        return carry

    lax.fori_loop(1, total, greet, 0)
    own = [
        pltpu.make_async_copy(source(a, me), outs[a].at[me], local.at[a]) for a in range(count)
    ]
    for one in own:
        one.start()
    pl.semaphore_wait(barrier, total - 1)
    lax.fori_loop(1, total, start, 0)
    for one in own:
        one.wait()
    lax.fori_loop(1, total, wait, 0)


def exchange(arrays, axes, sizes, collective_id):
    total = math.prod(sizes)
    blocks = tuple(array.shape[0] for array in arrays)
    anywhere = pl.BlockSpec(memory_space=pl.ANY)
    return pl.pallas_call(
        functools.partial(exchange_kernel, axes, sizes, blocks),
        in_specs=[anywhere] * len(arrays),
        out_specs=[anywhere] * len(arrays),
        out_shape=[
            jax.ShapeDtypeStruct((total,) + array.shape[1:], array.dtype) for array in arrays
        ],
        scratch_shapes=[
            pltpu.SemaphoreType.DMA((len(arrays), total)),
            pltpu.SemaphoreType.DMA((len(arrays), total)),
            pltpu.SemaphoreType.DMA((len(arrays),)),
        ],
        compiler_params=pltpu.CompilerParams(
            collective_id=collective_id, has_side_effects=True, vmem_limit_bytes=VMEM_LIMIT
        ),
        cost_estimate=pl.CostEstimate(
            flops=0, bytes_accessed=sum(8 * 2 * a.size for a in arrays), transcendentals=0
        ),
        name="exchange",
    )(*arrays)


def pad_planes(array, dim, spare):
    if not spare:
        return array
    return jnp.pad(array, [(0, spare if d == dim else 0) for d in range(array.ndim)])


def body(slabs, chans, field, cotangent, spectral_weight, point_weight, point_bias):
    channels, planes, cells = field.shape
    group = spectral_weight.shape[1]
    modes = spectral_weight.shape[3]
    own_planes = -(-planes // chans)
    spare = own_planes * chans - planes
    length = planes * slabs
    width = 2 * modes
    tiled = planes % 16 == 0 and own_planes % 8 == 0 and width % 128 == 0
    everyone = ("slab", "chan"), (slabs, chans)
    table = lax.optimization_barrier(jnp.asarray(plane_table(slabs)))
    cosine, sine = line_tables(length)
    lines = jnp.asarray(np.concatenate([cosine, sine], 1))
    lines_back = jnp.asarray(np.concatenate([cosine.T, sine.T], 1))
    turn, turn_back = jnp.asarray(turned(modes)), jnp.asarray(turned(modes).T)
    part, pack = jnp.asarray(part_of(modes)), jnp.asarray(np.swapaxes(part_of(modes), 1, 2))
    slab_index = lax.axis_index("slab")
    chan_index = lax.axis_index("chan")
    weight = jnp.swapaxes(spectral_weight, 3, 4)
    mode_index = slab_index * modes + jnp.arange(width, dtype=jnp.int32) % modes
    scale = (jnp.where(mode_index // MY == 0, 1.0, 2.0) / (length * cells)).astype(jnp.float32)
    scale = scale[None]

    if tiled:
        sections = begin(chan_index, field, table, group, slabs)
    else:
        own_field = lax.dynamic_slice_in_dim(field, chan_index * group, group, 0)
        sections = wide(own_field.reshape(group * planes, cells), table).astype(jnp.bfloat16)
        sections = jnp.moveaxis(sections.reshape(group * planes, slabs, width), 1, 0)
    (pencils,) = exchange([sections], ("slab",), (slabs,), 0)
    pencils = jnp.moveaxis(pencils.reshape(slabs, group, planes, width), 1, 0)
    partial, coeff = mix(
        pencils.reshape(group, length, width), lines, turn, part, pack, weight
    )
    (parts,) = exchange([partial.reshape(chans, group, MX, width)], ("chan",), (chans,), 1)
    pencils = spread(parts, scale, lines_back, turn_back)
    pencils = pad_planes(pencils.reshape(group, slabs, planes, width), 2, spare)
    pencils = pencils.reshape(group, slabs, chans, own_planes, width)
    pencils = jnp.transpose(pencils, (1, 2, 0, 3, 4))
    pencils = pencils.reshape(slabs * chans, group, own_planes, width)
    (slabs_in,) = exchange([pencils], *everyone, 4)
    slabs_in = slabs_in.reshape(slabs, channels, own_planes, width)
    rows = channels * own_planes
    slabs_in = jnp.transpose(slabs_in, (1, 2, 0, 3)).reshape(rows, slabs * width)

    own_index, own_field, own_cotangent = chan_index, field, cotangent
    if not tiled:
        own_index = jnp.zeros_like(chan_index)
        own_field, own_cotangent = (
            lax.dynamic_slice_in_dim(
                pad_planes(array, 1, spare), chan_index * own_planes, own_planes, 1
            )
            for array in (field, cotangent)
        )
    point, hat_rows, sums = grid_stage(
        own_index,
        slabs_in,
        table,
        own_field,
        own_cotangent,
        point_weight,
        jnp.repeat(point_bias.astype(jnp.float32), own_planes)[:, None],
        slabs if tiled else 1,
    )
    point = lax.all_to_all(
        point.reshape(chans, group, own_planes, cells),
        "chan", split_axis=0, concat_axis=0, tiled=True,
    )
    if not tiled:
        hat_rows = jnp.moveaxis(hat_rows.reshape(rows, slabs, width), 1, 0)
    hat_rows = hat_rows.reshape(slabs * chans, group, own_planes, width)
    own_sums = sums[:channels].reshape(chans, group, channels)
    bias_sums = jnp.broadcast_to(sums[channels:][None], (chans, 8, channels))
    own_sums = jnp.concatenate([own_sums, bias_sums], 1)
    pencils, all_sums = exchange([hat_rows, own_sums], *everyone, 2)
    pencils = jnp.moveaxis(pencils.reshape(slabs, chans, group, own_planes, width), 2, 0)
    pencils = pencils.reshape(group, slabs, chans * own_planes, width)[:, :, :planes]
    part_hat = gather_lines(pencils.reshape(group, length, width), scale, lines, turn)
    (hat,) = exchange([part_hat[None]], ("chan",), (chans,), 3)

    pencils, hat = adjoint_of(
        hat.reshape(channels, MX, width), lines_back, turn_back, part, pack, weight
    )
    pencils = pencils.reshape(group, slabs, planes, width)
    pencils, point = lax.optimization_barrier((pencils, point))
    (pencils,) = exchange([jnp.moveaxis(pencils, 1, 0)], ("slab",), (slabs,), 5)
    grad_spectral = jnp.swapaxes(outer(coeff, hat), 3, 4)
    pencils = jnp.moveaxis(pencils, 0, 2).reshape(group * planes, slabs * width)
    if tiled:
        grad_input = finish(pencils, table, point).reshape(group, planes, cells)
    else:
        back = lax.dot_general(pencils, table, ROWS_BY_ROWS, preferred_element_type=jnp.float32)
        back = back.reshape(group, planes, cells)
        point = jnp.moveaxis(point, 0, 1).reshape(group, chans * own_planes, cells)[:, :planes]
        grad_input = (back + point.astype(jnp.float32)).astype(jnp.bfloat16)

    sums = jnp.sum(all_sums, 0) * (1.0 / math.sqrt(length * cells))
    return (grad_input, grad_spectral, sums[:group], sums[group])


def solution(mesh):
    placed = (
        P(None, "slab", None),
        P(None, "slab", None),
        P(None, "chan", None, "slab", None),
        P(),
        P(),
    )
    return jax.shard_map(
        functools.partial(body, mesh.shape["slab"], mesh.shape["chan"]),
        mesh=mesh,
        in_specs=placed,
        out_specs=(
            P("chan", "slab", None),
            P(None, "chan", None, "slab", None),
            P("chan", None),
            P(),
        ),
        check_vma=False,
    )
```

```python
import functools
import math

import jax
import jax.numpy as jnp
import ml_dtypes
import numpy as np
from jax import lax
from jax.experimental import pallas as pl
from jax.experimental.pallas import tpu as pltpu
from jax.sharding import PartitionSpec as P

MX = 32
MY = 32
MZ = 16
NY = 64
NZ = 64

BF16 = ml_dtypes.bfloat16
VMEM_LIMIT = 50 * 1024 * 1024


def kept_modes(total, length):
    mode_index = np.arange(total, dtype=np.int32)
    return np.where(mode_index < total // 2, mode_index, mode_index - total + length)


def rounded_waves(frequency, length):
    positions = np.arange(length, dtype=np.int32)
    wound_up = frequency[:, None] * positions[None, :] % length
    angle = np.float32(2.0 * math.pi / length) * wound_up.astype(np.float32)
    cosine = np.cos(angle).astype(BF16).astype(np.float32)
    sine = np.sin(angle).astype(BF16).astype(np.float32)
    return cosine, sine


def plane_table(slabs):
    cosine_z, sine_z = rounded_waves(np.arange(MZ, dtype=np.int32), NZ)
    cosine_y, sine_y = rounded_waves(kept_modes(MY, NY), NY)
    cz, sz = cosine_z.T[None, :, :, None], sine_z.T[None, :, :, None]
    cy, sy = cosine_y.T[:, None, None, :], sine_y.T[:, None, None, :]
    real = (cz * cy - sz * sy).reshape(NY * NZ, slabs, 1, -1)
    imag = -(cz * sy + sz * cy).reshape(NY * NZ, slabs, 1, -1)
    return np.concatenate([real, imag], 2).reshape(NY * NZ, -1).astype(BF16)


def line_tables(length):
    cosine, sine = rounded_waves(kept_modes(MX, length), length)
    return cosine.astype(BF16), sine.astype(BF16)


def gelu_grad(pre_act):
    normal_cdf = 0.5 * (1.0 + lax.erf(pre_act * (1.0 / math.sqrt(2.0))))
    normal_pdf = jnp.exp(-0.5 * pre_act * pre_act) * (1.0 / math.sqrt(2.0 * math.pi))
    return normal_cdf + pre_act * normal_pdf


def params():
    return pltpu.CompilerParams(vmem_limit_bytes=VMEM_LIMIT)


def pick(total, wanted):
    return math.gcd(total, wanted)


def turned(modes):
    matrix = np.zeros((2 * modes, 2 * modes), np.float32)
    index = np.arange(modes)
    matrix[modes + index, index] = 1.0
    matrix[index, modes + index] = -1.0
    return matrix.astype(BF16)


def part_of(modes):
    matrix = np.zeros((2, 2 * modes, modes), np.float32)
    index = np.arange(modes)
    matrix[0, index, index] = 1.0
    matrix[1, modes + index, index] = 1.0
    return matrix.astype(BF16)


def wide(a, b):
    return jnp.dot(a, b, preferred_element_type=jnp.float32)


def line_modes(pencil, lines, turn):
    twisted = wide(pencil, turn).astype(jnp.bfloat16)
    return wide(lines, jnp.concatenate([pencil, twisted], 0))


def line_values(spectrum, lines_back, turn_back):
    twisted = wide(spectrum, turn_back).astype(jnp.bfloat16)
    return wide(lines_back, jnp.concatenate([spectrum, twisted], 0))


def whole(shape):
    return pl.BlockSpec(shape, lambda *_: (0,) * len(shape))


def mix_kernel(pencil_ref, lines_ref, turn_ref, part_ref, pack_ref, weight_ref, out_ref, coeff_ref, *, inner):
    group, outs = weight_ref.shape[1], weight_ref.shape[2]
    shape = weight_ref.shape[3:]

    @pl.when(pl.program_id(0) == 0)
    def _():
        def one_channel(i, carry):
            packed = line_modes(pencil_ref[i], lines_ref[...], turn_ref[...]).astype(jnp.bfloat16)
            coeff_ref[i, 0] = wide(packed, part_ref[0])
            coeff_ref[i, 1] = wide(packed, part_ref[1])
            return carry

        lax.fori_loop(0, group, one_channel, 0, unroll=4)

    def some_outputs(step, carry):
        first = step * inner

        def one_input(i, sums):
            real, imag = coeff_ref[i, 0], coeff_ref[i, 1]
            done = []
            for k in range(inner):
                wr = weight_ref[0, i, first + k].astype(jnp.float32)
                wi = weight_ref[1, i, first + k].astype(jnp.float32)
                done.append(sums[2 * k] + (real * wr - imag * wi))
                done.append(sums[2 * k + 1] + (real * wi + imag * wr))
            return tuple(done)

        zero = jnp.zeros(shape, jnp.float32)
        sums = lax.fori_loop(0, group, one_input, (zero,) * (2 * inner), unroll=4)
        for k in range(inner):
            out_ref[first + k] = (
                wide(sums[2 * k].astype(jnp.bfloat16), pack_ref[0])
                + wide(sums[2 * k + 1].astype(jnp.bfloat16), pack_ref[1])
            ).astype(out_ref.dtype)
        return carry

    lax.fori_loop(0, outs // inner, some_outputs, 0)


def mix(pencils, lines, turn, part, pack, weight):
    group, channels, kept, modes = weight.shape[1:]
    block = pick(channels, 8)
    return pl.pallas_call(
        functools.partial(mix_kernel, inner=pick(block, 4)),
        grid=(channels // block,),
        in_specs=[
            whole(pencils.shape), whole(lines.shape), whole(turn.shape), whole(part.shape),
            whole(pack.shape),
            pl.BlockSpec((2, group, block, kept, modes), lambda s: (0, 0, s, 0, 0)),
        ],
        out_specs=[
            pl.BlockSpec((block, kept, 2 * modes), lambda s: (s, 0, 0)),
            whole((group, 2, kept, modes)),
        ],
        out_shape=[
            jax.ShapeDtypeStruct((channels, kept, 2 * modes), jnp.bfloat16),
            jax.ShapeDtypeStruct((group, 2, kept, modes), jnp.float32),
        ],
        compiler_params=params(),
        cost_estimate=pl.CostEstimate(
            flops=4 * weight.size, bytes_accessed=4 * weight.size, transcendentals=0
        ),
        name="mix",
    )(pencils, lines, turn, part, pack, weight)


def spread_kernel(parts_ref, scale_ref, lines_ref, turn_ref, out_ref):
    def one_channel(i, carry):
        total = parts_ref[0, i].astype(jnp.float32)
        for g in range(1, parts_ref.shape[0]):
            total += parts_ref[g, i].astype(jnp.float32)
        spectrum = (total * scale_ref[...]).astype(jnp.bfloat16)
        out_ref[i] = line_values(spectrum, lines_ref[...], turn_ref[...]).astype(out_ref.dtype)
        return carry

    lax.fori_loop(0, parts_ref.shape[1], one_channel, 0, unroll=4)


def spread(parts, scale, lines, turn):
    group, width = parts.shape[1], parts.shape[3]
    shape = (group, lines.shape[0], width)
    return pl.pallas_call(
        spread_kernel,
        out_shape=jax.ShapeDtypeStruct(shape, jnp.bfloat16),
        compiler_params=params(),
        name="spread",
    )(parts, scale, lines, turn)


def gather_lines_kernel(pencil_ref, scale_ref, lines_ref, turn_ref, out_ref):
    def one_channel(i, carry):
        packed = line_modes(pencil_ref[i], lines_ref[...], turn_ref[...])
        out_ref[i] = (packed * scale_ref[...]).astype(out_ref.dtype)
        return carry

    lax.fori_loop(0, pencil_ref.shape[0], one_channel, 0, unroll=4)


def gather_lines(pencils, scale, lines, turn):
    shape = (pencils.shape[0], lines.shape[0], pencils.shape[2])
    return pl.pallas_call(
        gather_lines_kernel,
        out_shape=jax.ShapeDtypeStruct(shape, jnp.bfloat16),
        compiler_params=params(),
        name="lines",
    )(pencils, scale, lines, turn)


def adjoint_kernel(hat_ref, lines_ref, turn_ref, part_ref, pack_ref, weight_ref, out_ref, wide_ref):
    own, channels = weight_ref.shape[1], weight_ref.shape[2]
    shape = weight_ref.shape[3:]

    @pl.when(pl.program_id(0) == 0)
    def _():
        def one_channel(o, carry):
            wide_ref[o, 0] = wide(hat_ref[o], part_ref[0])
            wide_ref[o, 1] = wide(hat_ref[o], part_ref[1])
            return carry

        lax.fori_loop(0, channels, one_channel, 0, unroll=4)

    def one_output(o, sums):
        real, imag = wide_ref[o, 0], wide_ref[o, 1]
        done = []
        for k in range(own):
            wr = weight_ref[0, k, o].astype(jnp.float32)
            wi = weight_ref[1, k, o].astype(jnp.float32)
            done.append(sums[2 * k] + (real * wr + imag * wi))
            done.append(sums[2 * k + 1] + (imag * wr - real * wi))
        return tuple(done)

    zero = jnp.zeros(shape, jnp.float32)
    sums = lax.fori_loop(0, channels, one_output, (zero,) * (2 * own), unroll=4)
    for k in range(own):
        packed = wide(sums[2 * k].astype(jnp.bfloat16), pack_ref[0]) + wide(
            sums[2 * k + 1].astype(jnp.bfloat16), pack_ref[1]
        )
        values = line_values(packed.astype(jnp.bfloat16), lines_ref[...], turn_ref[...])
        out_ref[k] = values.astype(out_ref.dtype)


def adjoint_of(hat, lines, turn, part, pack, weight):
    group, channels, kept, modes = weight.shape[1:]
    block = pick(group, 2)
    length = lines.shape[0]
    return pl.pallas_call(
        adjoint_kernel,
        grid=(group // block,),
        in_specs=[
            whole(hat.shape), whole(lines.shape), whole(turn.shape), whole(part.shape),
            whole(pack.shape),
            pl.BlockSpec((2, block, channels, kept, modes), lambda s: (0, s, 0, 0, 0)),
        ],
        out_specs=[
            pl.BlockSpec((block, length, 2 * modes), lambda s: (s, 0, 0)),
            whole((channels, 2, kept, modes)),
        ],
        out_shape=[
            jax.ShapeDtypeStruct((group, length, 2 * modes), jnp.bfloat16),
            jax.ShapeDtypeStruct((channels, 2, kept, modes), jnp.float32),
        ],
        compiler_params=params(),
        cost_estimate=pl.CostEstimate(
            flops=4 * weight.size, bytes_accessed=4 * weight.size, transcendentals=0
        ),
        name="adjoint",
    )(hat, lines, turn, part, pack, weight)


def outer_kernel(coeff_ref, hat_ref, out_ref):
    own, channels = out_ref.shape[1], out_ref.shape[2]
    for i in range(own):
        cr, ci = coeff_ref[i, 0], coeff_ref[i, 1]

        def one_output(o, carry):
            hr, hi = hat_ref[o, 0], hat_ref[o, 1]
            out_ref[0, i, o] = cr * hr + ci * hi
            out_ref[1, i, o] = cr * hi - ci * hr
            return carry

        lax.fori_loop(0, channels, one_output, 0, unroll=4)


def outer(coeff, hat):
    group, _, lines, modes = coeff.shape
    channels = hat.shape[0]
    block = pick(group, 2)
    return pl.pallas_call(
        outer_kernel,
        grid=(group // block,),
        in_specs=[
            pl.BlockSpec((block, 2, lines, modes), lambda s: (s, 0, 0, 0)),
            pl.BlockSpec((channels, 2, lines, modes), lambda s: (0, 0, 0, 0)),
        ],
        out_specs=pl.BlockSpec((2, block, channels, lines, modes), lambda s: (0, s, 0, 0, 0)),
        out_shape=jax.ShapeDtypeStruct((2, group, channels, lines, modes), jnp.float32),
        compiler_params=params(),
        cost_estimate=pl.CostEstimate(
            flops=6 * group * channels * lines * modes,
            bytes_accessed=16 * group * channels * lines * modes,
            transcendentals=0,
        ),
        name="outer",
    )(coeff, hat)


ROWS_BY_ROWS = (((1,), (1,)), ((), ()))


def grid_kernel(
    chan_ref, modes_ref, table_ref, field_ref, cotangent_ref, point_weight_ref, repeat_ref, bias_ref,
    point_ref, hat_ref, sums_ref, total, weight_total, bias_total, mix_ref, back_ref, *, planes,
):
    step = pl.program_id(0)
    rows, channels = repeat_ref.shape

    def same_plane():
        first = lax.broadcasted_iota(jnp.int32, (rows, rows), 0) % planes
        return first == lax.broadcasted_iota(jnp.int32, (rows, rows), 1) % planes

    @pl.when(step == 0)
    def _():
        total[...] = jnp.zeros_like(total)
        weight_total[...] = jnp.zeros_like(weight_total)
        bias_total[...] = jnp.zeros_like(bias_total)
        repeat = repeat_ref[...]
        half = wide(repeat, point_weight_ref[...]).astype(jnp.bfloat16)
        full = lax.dot_general(half, repeat, ROWS_BY_ROWS, preferred_element_type=jnp.float32)
        back = jnp.where(same_plane(), full, 0.0)
        back_ref[...] = back.astype(jnp.bfloat16)
        mix_ref[...] = back.T.astype(jnp.bfloat16)

    table = table_ref[...]
    shape = (rows, field_ref.shape[-1])
    field = field_ref[...].astype(jnp.float32).reshape(shape).astype(jnp.bfloat16)
    pre_act = lax.dot_general(
        modes_ref[...], table, ROWS_BY_ROWS, preferred_element_type=jnp.float32
    )
    pre_act += jnp.dot(mix_ref[...], field, preferred_element_type=jnp.float32)
    pre_act += bias_ref[...]
    grad_wide = cotangent_ref[...].astype(jnp.float32).reshape(shape) * gelu_grad(pre_act)
    grad_pre = grad_wide.astype(jnp.bfloat16)
    point_ref[...] = jnp.dot(
        back_ref[...], grad_pre, preferred_element_type=jnp.float32
    ).astype(point_ref.dtype)
    total[...] += jnp.dot(grad_pre, table, preferred_element_type=jnp.float32)
    weight_total[...] += lax.dot_general(
        field, grad_pre, ROWS_BY_ROWS, preferred_element_type=jnp.float32
    )
    bias_total[...] += jnp.sum(grad_pre.astype(jnp.float32), axis=1, keepdims=True)

    @pl.when(step == pl.num_programs(0) - 1)
    def _():
        width = hat_ref.shape[-1]
        for s in range(hat_ref.shape[0]):
            hat_ref[s] = total[:, s * width : (s + 1) * width].astype(hat_ref.dtype)
        repeat = repeat_ref[...].astype(jnp.float32)
        kept = jnp.where(same_plane(), weight_total[...], 0.0)
        columns = jnp.dot(
            kept, repeat, precision=lax.Precision.HIGHEST, preferred_element_type=jnp.float32
        )
        both = (((0,), (0,)), ((), ()))
        sums_ref[:channels] = lax.dot_general(
            repeat, columns, both, precision=lax.Precision.HIGHEST,
            preferred_element_type=jnp.float32,
        )
        spread_bias = jnp.broadcast_to(bias_total[...], (rows, 8))
        sums_ref[channels:] = lax.dot_general(
            spread_bias, repeat, both, precision=lax.Precision.HIGHEST,
            preferred_element_type=jnp.float32,
        )


def grid_stage(chan_index, modes, table, field, cotangent, point_weight, bias, parts):
    rows, width = modes.shape
    cells = table.shape[0]
    channels = point_weight.shape[0]
    planes = rows // channels
    block = pick(cells, 512)
    repeat = jnp.asarray(np.repeat(np.eye(channels, dtype=np.float32), planes, 0).astype(BF16))
    own = pl.BlockSpec((channels, planes, block), lambda s, chan: (0, chan[0], s))
    return pl.pallas_call(
        functools.partial(grid_kernel, planes=planes),
        grid_spec=pltpu.PrefetchScalarGridSpec(
            num_scalar_prefetch=1,
            grid=(cells // block,),
            in_specs=[
                whole((rows, width)),
                pl.BlockSpec((block, width), lambda s, chan: (s, 0)),
                own,
                own,
                whole((channels, channels)),
                whole((rows, channels)),
                whole((rows, 1)),
            ],
            out_specs=[
                pl.BlockSpec((rows, block), lambda s, chan: (0, s)),
                whole((parts, rows, width // parts)),
                whole((channels + 8, channels)),
            ],
            scratch_shapes=[
                pltpu.VMEM((rows, width), jnp.float32),
                pltpu.VMEM((rows, rows), jnp.float32),
                pltpu.VMEM((rows, 1), jnp.float32),
                pltpu.VMEM((rows, rows), jnp.bfloat16),
                pltpu.VMEM((rows, rows), jnp.bfloat16),
            ],
        ),
        out_shape=[
            jax.ShapeDtypeStruct((rows, cells), jnp.bfloat16),
            jax.ShapeDtypeStruct((parts, rows, width // parts), jnp.bfloat16),
            jax.ShapeDtypeStruct((channels + 8, channels), jnp.float32),
        ],
        compiler_params=params(),
        cost_estimate=pl.CostEstimate(
            flops=2 * rows * cells * (2 * width + 3 * rows),
            bytes_accessed=2 * cells * (width + 3 * rows),
            transcendentals=2 * rows * cells,
        ),
        name="grid",
    )(chan_index.reshape(1), modes, table, field, cotangent, point_weight, repeat, bias)


def finish_kernel(chan_ref, modes_ref, table_ref, *refs):
    *point_refs, out_ref, point = refs
    chans = len(point_refs)
    for shift, point_ref in enumerate(point_refs):
        sender = lax.rem(chan_ref[0] + chans - shift, chans)
        point[sender] = point_ref[...].astype(jnp.float32).reshape(point.shape[1:])
    back = lax.dot_general(
        modes_ref[...], table_ref[...], ROWS_BY_ROWS, preferred_element_type=jnp.float32
    )
    sums = back + jnp.swapaxes(point[...], 0, 1).reshape(back.shape)
    out_ref[...] = sums.astype(out_ref.dtype)


def finish(chan_index, modes, table, points):
    group, planes, cells = points[0].shape
    chans = len(points)
    rows, width = modes.shape
    block = pick(cells, 512)
    return pl.pallas_call(
        finish_kernel,
        grid_spec=pltpu.PrefetchScalarGridSpec(
            num_scalar_prefetch=1,
            grid=(cells // block,),
            in_specs=[
                whole((rows, width)),
                pl.BlockSpec((block, width), lambda s, chan: (s, 0)),
            ] + [pl.BlockSpec((group, planes, block), lambda s, chan: (0, 0, s))] * chans,
            out_specs=pl.BlockSpec((rows, block), lambda s, chan: (0, s)),
            scratch_shapes=[pltpu.VMEM((chans, group, planes, block), jnp.float32)],
        ),
        out_shape=jax.ShapeDtypeStruct((rows, cells), jnp.bfloat16),
        compiler_params=params(),
        cost_estimate=pl.CostEstimate(
            flops=2 * rows * cells * width,
            bytes_accessed=2 * cells * (width + 2 * rows),
            transcendentals=0,
        ),
        name="finish",
    )(chan_index.reshape(1), modes, table, *points)


def begin_kernel(chan_ref, field_ref, table_ref, out_ref, total):
    step = pl.program_id(0)
    field = field_ref[...].reshape(total.shape[0], field_ref.shape[2])
    part = wide(field, table_ref[...])

    @pl.when(step == 0)
    def _():
        total[...] = part

    @pl.when(step > 0)
    def _():
        total[...] += part

    @pl.when(step == pl.num_programs(0) - 1)
    def _():
        width = out_ref.shape[-1]
        for s in range(out_ref.shape[0]):
            out_ref[s] = total[:, s * width : (s + 1) * width].astype(out_ref.dtype)


def begin(chan_index, field, table, group, parts):
    planes, cells = field.shape[1:]
    width = table.shape[1]
    rows = group * planes
    block = pick(cells, 1024)
    return pl.pallas_call(
        begin_kernel,
        grid_spec=pltpu.PrefetchScalarGridSpec(
            num_scalar_prefetch=1,
            grid=(cells // block,),
            in_specs=[
                pl.BlockSpec((group, planes, block), lambda s, chan: (chan[0], 0, s)),
                pl.BlockSpec((block, width), lambda s, chan: (s, 0)),
            ],
            out_specs=whole((parts, rows, width // parts)),
            scratch_shapes=[pltpu.VMEM((rows, width), jnp.float32)],
        ),
        out_shape=jax.ShapeDtypeStruct((parts, rows, width // parts), jnp.bfloat16),
        compiler_params=params(),
        cost_estimate=pl.CostEstimate(
            flops=2 * rows * cells * width,
            bytes_accessed=2 * cells * (width + rows),
            transcendentals=0,
        ),
        name="begin",
    )(chan_index.reshape(1), field, table)


def exchange_kernel(axes, sizes, blocks, *refs):
    count = len(blocks)
    ins, outs = refs[:count], refs[count : 2 * count]
    send, recv, local = refs[2 * count :]
    total = math.prod(sizes)
    last = sizes[-1]
    me = lax.axis_index(axes[0])
    if len(axes) == 2:
        me = me * last + lax.axis_index(axes[1])

    def place(index):
        if len(axes) == 2:
            return {axes[0]: lax.div(index, last), axes[1]: lax.rem(index, last)}
        return {axes[0]: index}

    def source(a, index):
        if blocks[a] == total:
            return ins[a].at[index]
        if blocks[a] == 1:
            return ins[a].at[0]
        return ins[a].at[lax.rem(index, last)]

    def copy(a, shift):
        peer = lax.rem(me + shift, total)
        return pltpu.make_async_remote_copy(
            src_ref=source(a, peer),
            dst_ref=outs[a].at[me],
            send_sem=send.at[a, shift],
            recv_sem=recv.at[a, shift],
            device_id=place(peer),
            device_id_type=pl.DeviceIdType.MESH,
        )

    barrier = pltpu.get_barrier_semaphore()

    def greet(shift, carry):
        pl.semaphore_signal(
            barrier, inc=1, device_id=place(lax.rem(me + shift, total)),
            device_id_type=pl.DeviceIdType.MESH,
        )
        return carry

    def start(shift, carry):
        for a in range(count):
            copy(a, shift).start()
        return carry

    def wait(shift, carry):
        for a in range(count):
            copy(a, shift).wait()
        return carry

    lax.fori_loop(1, total, greet, 0)
    own = [
        pltpu.make_async_copy(source(a, me), outs[a].at[me], local.at[a]) for a in range(count)
    ]
    for one in own:
        one.start()
    pl.semaphore_wait(barrier, total - 1)
    lax.fori_loop(1, total, start, 0)
    for one in own:
        one.wait()
    lax.fori_loop(1, total, wait, 0)


def exchange(arrays, axes, sizes, collective_id):
    total = math.prod(sizes)
    blocks = tuple(array.shape[0] for array in arrays)
    anywhere = pl.BlockSpec(memory_space=pl.ANY)
    return pl.pallas_call(
        functools.partial(exchange_kernel, axes, sizes, blocks),
        in_specs=[anywhere] * len(arrays),
        out_specs=[anywhere] * len(arrays),
        out_shape=[
            jax.ShapeDtypeStruct((total,) + array.shape[1:], array.dtype) for array in arrays
        ],
        scratch_shapes=[
            pltpu.SemaphoreType.DMA((len(arrays), total)),
            pltpu.SemaphoreType.DMA((len(arrays), total)),
            pltpu.SemaphoreType.DMA((len(arrays),)),
        ],
        compiler_params=pltpu.CompilerParams(
            collective_id=collective_id, has_side_effects=True, vmem_limit_bytes=VMEM_LIMIT
        ),
        cost_estimate=pl.CostEstimate(
            flops=0, bytes_accessed=sum(2 * a.size for a in arrays), transcendentals=0
        ),
        name="exchange",
    )(*arrays)


def pad_planes(array, dim, spare):
    if not spare:
        return array
    return jnp.pad(array, [(0, spare if d == dim else 0) for d in range(array.ndim)])


def body(slabs, chans, field, cotangent, spectral_weight, point_weight, point_bias):
    channels, planes, cells = field.shape
    group = spectral_weight.shape[1]
    modes = spectral_weight.shape[3]
    own_planes = -(-planes // chans)
    spare = own_planes * chans - planes
    length = planes * slabs
    width = 2 * modes
    tiled = planes % 16 == 0 and own_planes % 8 == 0 and width % 128 == 0
    everyone = ("slab", "chan"), (slabs, chans)
    table = lax.optimization_barrier(jnp.asarray(plane_table(slabs)))
    cosine, sine = line_tables(length)
    lines = jnp.asarray(np.concatenate([cosine, sine], 1))
    lines_back = jnp.asarray(np.concatenate([cosine.T, sine.T], 1))
    turn, turn_back = jnp.asarray(turned(modes)), jnp.asarray(turned(modes).T)
    part, pack = jnp.asarray(part_of(modes)), jnp.asarray(np.swapaxes(part_of(modes), 1, 2))
    slab_index = lax.axis_index("slab")
    chan_index = lax.axis_index("chan")
    weight = jnp.swapaxes(spectral_weight, 3, 4)
    mode_index = slab_index * modes + jnp.arange(width, dtype=jnp.int32) % modes
    scale = (jnp.where(mode_index // MY == 0, 1.0, 2.0) / (length * cells)).astype(jnp.float32)
    scale = scale[None]

    if tiled:
        sections = begin(chan_index, field, table, group, slabs)
    else:
        own_field = lax.dynamic_slice_in_dim(field, chan_index * group, group, 0)
        sections = wide(own_field.reshape(group * planes, cells), table).astype(jnp.bfloat16)
        sections = jnp.moveaxis(sections.reshape(group * planes, slabs, width), 1, 0)
    (pencils,) = exchange([sections], ("slab",), (slabs,), 0)
    pencils = jnp.moveaxis(pencils.reshape(slabs, group, planes, width), 1, 0)
    partial, coeff = mix(
        pencils.reshape(group, length, width), lines, turn, part, pack, weight
    )
    (parts,) = exchange([partial.reshape(chans, group, MX, width)], ("chan",), (chans,), 1)
    pencils = spread(parts, scale, lines_back, turn_back)
    pencils = pad_planes(pencils.reshape(group, slabs, planes, width), 2, spare)
    pencils = pencils.reshape(group, slabs, chans, own_planes, width)
    pencils = jnp.transpose(pencils, (1, 2, 0, 3, 4))
    pencils = pencils.reshape(slabs * chans, group, own_planes, width)
    (slabs_in,) = exchange([pencils], *everyone, 4)
    slabs_in = slabs_in.reshape(slabs, channels, own_planes, width)
    rows = channels * own_planes
    slabs_in = jnp.transpose(slabs_in, (1, 2, 0, 3)).reshape(rows, slabs * width)

    own_index, own_field, own_cotangent = chan_index, field, cotangent
    if not tiled:
        own_index = jnp.zeros_like(chan_index)
        own_field, own_cotangent = (
            lax.dynamic_slice_in_dim(
                pad_planes(array, 1, spare), chan_index * own_planes, own_planes, 1
            )
            for array in (field, cotangent)
        )
    point, hat_rows, sums = grid_stage(
        own_index,
        slabs_in,
        table,
        own_field,
        own_cotangent,
        point_weight,
        jnp.repeat(point_bias.astype(jnp.float32), own_planes)[:, None],
        slabs if tiled else 1,
    )
    if not tiled:
        hat_rows = jnp.moveaxis(hat_rows.reshape(rows, slabs, width), 1, 0)
    hat_rows = hat_rows.reshape(slabs * chans, group, own_planes, width)
    own_sums = sums[:channels].reshape(chans, group, channels)
    bias_sums = jnp.broadcast_to(sums[channels:][None], (chans, 8, channels))
    own_sums = jnp.concatenate([own_sums, bias_sums], 1)
    pencils, all_sums = exchange([hat_rows, own_sums], *everyone, 2)
    pencils = jnp.moveaxis(pencils.reshape(slabs, chans, group, own_planes, width), 2, 0)
    pencils = pencils.reshape(group, slabs, chans * own_planes, width)[:, :, :planes]
    part_hat = gather_lines(pencils.reshape(group, length, width), scale, lines, turn)
    (hat,) = exchange([part_hat[None]], ("chan",), (chans,), 3)
    hat, point = lax.optimization_barrier((hat, point))
    point = point.reshape(chans, group, own_planes, cells)
    points = []
    for shift in range(chans):
        receiver = (chan_index + shift) % chans
        block = lax.dynamic_index_in_dim(point, receiver, 0, keepdims=False)
        if shift:
            block = lax.ppermute(block, "chan", [(c, (c + shift) % chans) for c in range(chans)])
        points.append(block)

    pencils, hat = adjoint_of(
        hat.reshape(channels, MX, width), lines_back, turn_back, part, pack, weight
    )
    pencils = pencils.reshape(group, slabs, planes, width)
    (pencils,) = exchange([jnp.moveaxis(pencils, 1, 0)], ("slab",), (slabs,), 5)
    grad_spectral = jnp.swapaxes(outer(coeff, hat), 3, 4)
    pencils = jnp.moveaxis(pencils, 0, 2).reshape(group * planes, slabs * width)
    if tiled:
        grad_input = finish(chan_index, pencils, table, points).reshape(group, planes, cells)
    else:
        back = lax.dot_general(pencils, table, ROWS_BY_ROWS, preferred_element_type=jnp.float32)
        back = back.reshape(group, planes, cells)
        order = (chan_index - jnp.arange(chans)) % chans
        point = jnp.take(jnp.stack(points), order, axis=0)
        point = jnp.moveaxis(point, 0, 1).reshape(group, chans * own_planes, cells)[:, :planes]
        grad_input = (back + point.astype(jnp.float32)).astype(jnp.bfloat16)

    sums = jnp.sum(all_sums, 0) * (1.0 / math.sqrt(length * cells))
    return (grad_input, grad_spectral, sums[:group], sums[group])


def solution(mesh):
    placed = (
        P(None, "slab", None),
        P(None, "slab", None),
        P(None, "chan", None, "slab", None),
        P(),
        P(),
    )
    return jax.shard_map(
        functools.partial(body, mesh.shape["slab"], mesh.shape["chan"]),
        mesh=mesh,
        in_specs=placed,
        out_specs=(
            P("chan", "slab", None),
            P(None, "chan", None, "slab", None),
            P("chan", None),
            P(),
        ),
        check_vma=False,
    )
```

```python
import functools
import math

import jax
import jax.numpy as jnp
import ml_dtypes
import numpy as np
from jax import lax
from jax.experimental import pallas as pl
from jax.experimental.pallas import tpu as pltpu
from jax.sharding import PartitionSpec as P

MX = 32
MY = 32
MZ = 16
NY = 64
NZ = 64

BF16 = ml_dtypes.bfloat16
VMEM_LIMIT = 50 * 1024 * 1024


def kept_modes(total, length):
    mode_index = np.arange(total, dtype=np.int32)
    return np.where(mode_index < total // 2, mode_index, mode_index - total + length)


def rounded_waves(frequency, length):
    positions = np.arange(length, dtype=np.int32)
    wound_up = frequency[:, None] * positions[None, :] % length
    angle = np.float32(2.0 * math.pi / length) * wound_up.astype(np.float32)
    cosine = np.cos(angle).astype(BF16).astype(np.float32)
    sine = np.sin(angle).astype(BF16).astype(np.float32)
    return cosine, sine


def plane_table(slabs):
    cosine_z, sine_z = rounded_waves(np.arange(MZ, dtype=np.int32), NZ)
    cosine_y, sine_y = rounded_waves(kept_modes(MY, NY), NY)
    cz, sz = cosine_z.T[None, :, :, None], sine_z.T[None, :, :, None]
    cy, sy = cosine_y.T[:, None, None, :], sine_y.T[:, None, None, :]
    real = (cz * cy - sz * sy).reshape(NY * NZ, slabs, 1, -1)
    imag = -(cz * sy + sz * cy).reshape(NY * NZ, slabs, 1, -1)
    return np.concatenate([real, imag], 2).reshape(NY * NZ, -1).astype(BF16)


def line_tables(length):
    cosine, sine = rounded_waves(kept_modes(MX, length), length)
    return cosine.astype(BF16), sine.astype(BF16)


def gelu_grad(pre_act):
    normal_cdf = 0.5 * (1.0 + lax.erf(pre_act * (1.0 / math.sqrt(2.0))))
    normal_pdf = jnp.exp(-0.5 * pre_act * pre_act) * (1.0 / math.sqrt(2.0 * math.pi))
    return normal_cdf + pre_act * normal_pdf


def params():
    return pltpu.CompilerParams(vmem_limit_bytes=VMEM_LIMIT)


def pick(total, wanted):
    return math.gcd(total, wanted)


def turned(modes):
    matrix = np.zeros((2 * modes, 2 * modes), np.float32)
    index = np.arange(modes)
    matrix[modes + index, index] = 1.0
    matrix[index, modes + index] = -1.0
    return matrix.astype(BF16)


def part_of(modes):
    matrix = np.zeros((2, 2, modes, 2, modes), np.float32)
    index = np.arange(modes)
    for part in range(2):
        matrix[part, part, index, :, index] = 1.0
    return matrix.reshape(2, 2 * modes, 2 * modes).astype(BF16)


def pack_of(modes):
    matrix = np.zeros((2, 2, 2, modes, 2, modes), np.float32)
    index = np.arange(modes)
    for half in range(2):
        for part in range(2):
            matrix[half, part, half, index, part, index] = 1.0
    return matrix.reshape(2, 2, 2 * modes, 2 * modes).astype(BF16)


def wide(a, b):
    return jnp.dot(a, b, preferred_element_type=jnp.float32)


def line_modes(pencil, lines, turn):
    twisted = wide(pencil, turn).astype(jnp.bfloat16)
    return wide(lines, jnp.concatenate([pencil, twisted], 0))


def line_values(spectrum, lines_back, turn_back):
    twisted = wide(spectrum, turn_back).astype(jnp.bfloat16)
    return wide(lines_back, jnp.concatenate([spectrum, twisted], 0))


def side_by_side(first, second):
    return jnp.concatenate([first, second], 1).astype(jnp.float32)


def packed_half(real, imag, pack_ref, half):
    return wide(real.astype(jnp.bfloat16), pack_ref[half, 0]) + wide(
        imag.astype(jnp.bfloat16), pack_ref[half, 1]
    )


def whole(shape):
    return pl.BlockSpec(shape, lambda *_: (0,) * len(shape))


def mix_kernel(pencil_ref, lines_ref, turn_ref, part_ref, pack_ref, weight_ref, out_ref, coeff_ref, *, inner):
    group, outs, kept, modes = weight_ref.shape[1:]
    shape = (kept, 2 * modes)

    @pl.when(pl.program_id(0) == 0)
    def _():
        def one_channel(i, carry):
            packed = line_modes(pencil_ref[i], lines_ref[...], turn_ref[...]).astype(jnp.bfloat16)
            coeff_ref[i, 0] = wide(packed, part_ref[0])
            coeff_ref[i, 1] = wide(packed, part_ref[1])
            return carry

        lax.fori_loop(0, group, one_channel, 0, unroll=4)

    def some_outputs(step, carry):
        first = step * inner

        def one_input(i, sums):
            real, imag = coeff_ref[i, 0], coeff_ref[i, 1]
            done = []
            for k in range(inner // 2):
                pair = first + 2 * k
                wr = side_by_side(weight_ref[0, i, pair], weight_ref[0, i, pair + 1])
                wi = side_by_side(weight_ref[1, i, pair], weight_ref[1, i, pair + 1])
                done.append(sums[2 * k] + (real * wr - imag * wi))
                done.append(sums[2 * k + 1] + (real * wi + imag * wr))
            return tuple(done)

        zero = jnp.zeros(shape, jnp.float32)
        sums = lax.fori_loop(0, group, one_input, (zero,) * inner, unroll=2)
        for k in range(inner):
            pair = 2 * (k // 2)
            out_ref[first + k] = packed_half(
                sums[pair], sums[pair + 1], pack_ref, k % 2
            ).astype(out_ref.dtype)
        return carry

    lax.fori_loop(0, outs // inner, some_outputs, 0)


def mix(pencils, lines, turn, part, pack, weight):
    group, channels, kept, modes = weight.shape[1:]
    block = pick(channels, 8)
    return pl.pallas_call(
        functools.partial(mix_kernel, inner=pick(block, 4)),
        grid=(channels // block,),
        in_specs=[
            whole(pencils.shape), whole(lines.shape), whole(turn.shape), whole(part.shape),
            whole(pack.shape),
            pl.BlockSpec((2, group, block, kept, modes), lambda s: (0, 0, s, 0, 0)),
        ],
        out_specs=[
            pl.BlockSpec((block, kept, 2 * modes), lambda s: (s, 0, 0)),
            whole((group, 2, kept, 2 * modes)),
        ],
        out_shape=[
            jax.ShapeDtypeStruct((channels, kept, 2 * modes), jnp.bfloat16),
            jax.ShapeDtypeStruct((group, 2, kept, 2 * modes), jnp.float32),
        ],
        compiler_params=params(),
        cost_estimate=pl.CostEstimate(
            flops=4 * weight.size, bytes_accessed=4 * weight.size, transcendentals=0
        ),
        name="mix",
    )(pencils, lines, turn, part, pack, weight)


def spread_kernel(parts_ref, scale_ref, lines_ref, turn_ref, out_ref):
    def one_channel(i, carry):
        total = parts_ref[0, i].astype(jnp.float32)
        for g in range(1, parts_ref.shape[0]):
            total += parts_ref[g, i].astype(jnp.float32)
        spectrum = (total * scale_ref[...]).astype(jnp.bfloat16)
        out_ref[i] = line_values(spectrum, lines_ref[...], turn_ref[...]).astype(out_ref.dtype)
        return carry

    lax.fori_loop(0, parts_ref.shape[1], one_channel, 0, unroll=4)


def spread(parts, scale, lines, turn):
    group, width = parts.shape[1], parts.shape[3]
    shape = (group, lines.shape[0], width)
    return pl.pallas_call(
        spread_kernel,
        out_shape=jax.ShapeDtypeStruct(shape, jnp.bfloat16),
        compiler_params=params(),
        name="spread",
    )(parts, scale, lines, turn)


def gather_lines_kernel(pencil_ref, scale_ref, lines_ref, turn_ref, out_ref):
    def one_channel(i, carry):
        packed = line_modes(pencil_ref[i], lines_ref[...], turn_ref[...])
        out_ref[i] = (packed * scale_ref[...]).astype(out_ref.dtype)
        return carry

    lax.fori_loop(0, pencil_ref.shape[0], one_channel, 0, unroll=4)


def gather_lines(pencils, scale, lines, turn):
    shape = (pencils.shape[0], lines.shape[0], pencils.shape[2])
    return pl.pallas_call(
        gather_lines_kernel,
        out_shape=jax.ShapeDtypeStruct(shape, jnp.bfloat16),
        compiler_params=params(),
        name="lines",
    )(pencils, scale, lines, turn)


def adjoint_kernel(hat_ref, lines_ref, turn_ref, part_ref, pack_ref, weight_ref, out_ref, wide_ref):
    own, channels, kept, modes = weight_ref.shape[1:]
    shape = (kept, 2 * modes)

    @pl.when(pl.program_id(0) == 0)
    def _():
        def one_channel(o, carry):
            wide_ref[o, 0] = wide(hat_ref[o], part_ref[0])
            wide_ref[o, 1] = wide(hat_ref[o], part_ref[1])
            return carry

        lax.fori_loop(0, channels, one_channel, 0, unroll=4)

    def one_output(o, sums):
        real, imag = wide_ref[o, 0], wide_ref[o, 1]
        done = []
        for k in range(0, own, 2):
            wr = side_by_side(weight_ref[0, k, o], weight_ref[0, k + 1, o])
            wi = side_by_side(weight_ref[1, k, o], weight_ref[1, k + 1, o])
            done.append(sums[k] + (real * wr + imag * wi))
            done.append(sums[k + 1] + (imag * wr - real * wi))
        return tuple(done)

    zero = jnp.zeros(shape, jnp.float32)
    sums = lax.fori_loop(0, channels, one_output, (zero,) * own, unroll=4)
    for k in range(own):
        pair = 2 * (k // 2)
        packed = packed_half(sums[pair], sums[pair + 1], pack_ref, k % 2)
        values = line_values(packed.astype(jnp.bfloat16), lines_ref[...], turn_ref[...])
        out_ref[k] = values.astype(out_ref.dtype)


def adjoint_of(hat, lines, turn, part, pack, weight):
    group, channels, kept, modes = weight.shape[1:]
    block = pick(group, 2)
    length = lines.shape[0]
    return pl.pallas_call(
        adjoint_kernel,
        grid=(group // block,),
        in_specs=[
            whole(hat.shape), whole(lines.shape), whole(turn.shape), whole(part.shape),
            whole(pack.shape),
            pl.BlockSpec((2, block, channels, kept, modes), lambda s: (0, s, 0, 0, 0)),
        ],
        out_specs=[
            pl.BlockSpec((block, length, 2 * modes), lambda s: (s, 0, 0)),
            whole((channels, 2, kept, 2 * modes)),
        ],
        out_shape=[
            jax.ShapeDtypeStruct((group, length, 2 * modes), jnp.bfloat16),
            jax.ShapeDtypeStruct((channels, 2, kept, 2 * modes), jnp.float32),
        ],
        compiler_params=params(),
        cost_estimate=pl.CostEstimate(
            flops=4 * weight.size, bytes_accessed=4 * weight.size, transcendentals=0
        ),
        name="adjoint",
    )(hat, lines, turn, part, pack, weight)


def outer_kernel(coeff_ref, hat_ref, out_ref):
    own, channels = out_ref.shape[1], out_ref.shape[2]
    for i in range(own):
        cr, ci = coeff_ref[i, 0], coeff_ref[i, 1]

        def one_output(o, carry):
            hr, hi = hat_ref[o, 0], hat_ref[o, 1]
            modes = out_ref.shape[-1]
            out_ref[0, i, o] = (cr * hr + ci * hi)[:, :modes]
            out_ref[1, i, o] = (cr * hi - ci * hr)[:, :modes]
            return carry

        lax.fori_loop(0, channels, one_output, 0, unroll=4)


def outer(coeff, hat):
    group, _, lines, width = coeff.shape
    modes = width // 2
    channels = hat.shape[0]
    block = pick(group, 2)
    return pl.pallas_call(
        outer_kernel,
        grid=(group // block,),
        in_specs=[
            pl.BlockSpec((block, 2, lines, width), lambda s: (s, 0, 0, 0)),
            pl.BlockSpec((channels, 2, lines, width), lambda s: (0, 0, 0, 0)),
        ],
        out_specs=pl.BlockSpec((2, block, channels, lines, modes), lambda s: (0, s, 0, 0, 0)),
        out_shape=jax.ShapeDtypeStruct((2, group, channels, lines, modes), jnp.float32),
        compiler_params=params(),
        cost_estimate=pl.CostEstimate(
            flops=6 * group * channels * lines * modes,
            bytes_accessed=16 * group * channels * lines * modes,
            transcendentals=0,
        ),
        name="outer",
    )(coeff, hat)


ROWS_BY_ROWS = (((1,), (1,)), ((), ()))


def grid_kernel(
    chan_ref, modes_ref, table_ref, field_ref, cotangent_ref, point_weight_ref, repeat_ref, bias_ref,
    point_ref, hat_ref, sums_ref, total, weight_total, bias_total, mix_ref, back_ref, *, planes,
):
    step = pl.program_id(0)
    rows, channels = repeat_ref.shape

    def same_plane():
        first = lax.broadcasted_iota(jnp.int32, (rows, rows), 0) % planes
        return first == lax.broadcasted_iota(jnp.int32, (rows, rows), 1) % planes

    @pl.when(step == 0)
    def _():
        total[...] = jnp.zeros_like(total)
        weight_total[...] = jnp.zeros_like(weight_total)
        bias_total[...] = jnp.zeros_like(bias_total)
        repeat = repeat_ref[...]
        half = wide(repeat, point_weight_ref[...]).astype(jnp.bfloat16)
        full = lax.dot_general(half, repeat, ROWS_BY_ROWS, preferred_element_type=jnp.float32)
        back = jnp.where(same_plane(), full, 0.0)
        back_ref[...] = back.astype(jnp.bfloat16)
        mix_ref[...] = back.T.astype(jnp.bfloat16)

    table = table_ref[...]
    shape = (rows, field_ref.shape[-1])
    field = field_ref[...].astype(jnp.float32).reshape(shape).astype(jnp.bfloat16)
    pre_act = lax.dot_general(
        modes_ref[...], table, ROWS_BY_ROWS, preferred_element_type=jnp.float32
    )
    pre_act += jnp.dot(mix_ref[...], field, preferred_element_type=jnp.float32)
    pre_act += bias_ref[...]
    grad_wide = cotangent_ref[...].astype(jnp.float32).reshape(shape) * gelu_grad(pre_act)
    grad_pre = grad_wide.astype(jnp.bfloat16)
    point_ref[...] = jnp.dot(
        back_ref[...], grad_pre, preferred_element_type=jnp.float32
    ).astype(point_ref.dtype)
    total[...] += jnp.dot(grad_pre, table, preferred_element_type=jnp.float32)
    weight_total[...] += lax.dot_general(
        field, grad_pre, ROWS_BY_ROWS, preferred_element_type=jnp.float32
    )
    bias_total[...] += jnp.sum(grad_pre.astype(jnp.float32), axis=1, keepdims=True)

    @pl.when(step == pl.num_programs(0) - 1)
    def _():
        width = hat_ref.shape[-1]
        for s in range(hat_ref.shape[0]):
            hat_ref[s] = total[:, s * width : (s + 1) * width].astype(hat_ref.dtype)
        repeat = repeat_ref[...].astype(jnp.float32)
        kept = jnp.where(same_plane(), weight_total[...], 0.0)
        columns = jnp.dot(
            kept, repeat, precision=lax.Precision.HIGHEST, preferred_element_type=jnp.float32
        )
        both = (((0,), (0,)), ((), ()))
        sums_ref[:channels] = lax.dot_general(
            repeat, columns, both, precision=lax.Precision.HIGHEST,
            preferred_element_type=jnp.float32,
        )
        spread_bias = jnp.broadcast_to(bias_total[...], (rows, 8))
        sums_ref[channels:] = lax.dot_general(
            spread_bias, repeat, both, precision=lax.Precision.HIGHEST,
            preferred_element_type=jnp.float32,
        )


def grid_stage(chan_index, modes, table, field, cotangent, point_weight, bias, parts):
    rows, width = modes.shape
    cells = table.shape[0]
    channels = point_weight.shape[0]
    planes = rows // channels
    block = pick(cells, 512)
    repeat = jnp.asarray(np.repeat(np.eye(channels, dtype=np.float32), planes, 0).astype(BF16))
    own = pl.BlockSpec((channels, planes, block), lambda s, chan: (0, chan[0], s))
    return pl.pallas_call(
        functools.partial(grid_kernel, planes=planes),
        grid_spec=pltpu.PrefetchScalarGridSpec(
            num_scalar_prefetch=1,
            grid=(cells // block,),
            in_specs=[
                whole((rows, width)),
                pl.BlockSpec((block, width), lambda s, chan: (s, 0)),
                own,
                own,
                whole((channels, channels)),
                whole((rows, channels)),
                whole((rows, 1)),
            ],
            out_specs=[
                pl.BlockSpec((rows, block), lambda s, chan: (0, s)),
                whole((parts, rows, width // parts)),
                whole((channels + 8, channels)),
            ],
            scratch_shapes=[
                pltpu.VMEM((rows, width), jnp.float32),
                pltpu.VMEM((rows, rows), jnp.float32),
                pltpu.VMEM((rows, 1), jnp.float32),
                pltpu.VMEM((rows, rows), jnp.bfloat16),
                pltpu.VMEM((rows, rows), jnp.bfloat16),
            ],
        ),
        out_shape=[
            jax.ShapeDtypeStruct((rows, cells), jnp.bfloat16),
            jax.ShapeDtypeStruct((parts, rows, width // parts), jnp.bfloat16),
            jax.ShapeDtypeStruct((channels + 8, channels), jnp.float32),
        ],
        compiler_params=params(),
        cost_estimate=pl.CostEstimate(
            flops=2 * rows * cells * (2 * width + 3 * rows),
            bytes_accessed=2 * cells * (width + 3 * rows),
            transcendentals=2 * rows * cells,
        ),
        name="grid",
    )(chan_index.reshape(1), modes, table, field, cotangent, point_weight, repeat, bias)


def finish_kernel(chan_ref, modes_ref, table_ref, *refs):
    *point_refs, out_ref, point = refs
    chans = len(point_refs)
    for shift, point_ref in enumerate(point_refs):
        sender = lax.rem(chan_ref[0] + chans - shift, chans)
        point[sender] = point_ref[...].astype(jnp.float32).reshape(point.shape[1:])
    back = lax.dot_general(
        modes_ref[...], table_ref[...], ROWS_BY_ROWS, preferred_element_type=jnp.float32
    )
    sums = back + jnp.swapaxes(point[...], 0, 1).reshape(back.shape)
    out_ref[...] = sums.astype(out_ref.dtype)


def finish(chan_index, modes, table, points):
    group, planes, cells = points[0].shape
    chans = len(points)
    rows, width = modes.shape
    block = pick(cells, 512)
    return pl.pallas_call(
        finish_kernel,
        grid_spec=pltpu.PrefetchScalarGridSpec(
            num_scalar_prefetch=1,
            grid=(cells // block,),
            in_specs=[
                whole((rows, width)),
                pl.BlockSpec((block, width), lambda s, chan: (s, 0)),
            ] + [pl.BlockSpec((group, planes, block), lambda s, chan: (0, 0, s))] * chans,
            out_specs=pl.BlockSpec((rows, block), lambda s, chan: (0, s)),
            scratch_shapes=[pltpu.VMEM((chans, group, planes, block), jnp.float32)],
        ),
        out_shape=jax.ShapeDtypeStruct((rows, cells), jnp.bfloat16),
        compiler_params=params(),
        cost_estimate=pl.CostEstimate(
            flops=2 * rows * cells * width,
            bytes_accessed=2 * cells * (width + 2 * rows),
            transcendentals=0,
        ),
        name="finish",
    )(chan_index.reshape(1), modes, table, *points)


def begin_kernel(chan_ref, field_ref, table_ref, out_ref, total):
    step = pl.program_id(0)
    field = field_ref[...].reshape(total.shape[0], field_ref.shape[2])
    part = wide(field, table_ref[...])

    @pl.when(step == 0)
    def _():
        total[...] = part

    @pl.when(step > 0)
    def _():
        total[...] += part

    @pl.when(step == pl.num_programs(0) - 1)
    def _():
        width = out_ref.shape[-1]
        for s in range(out_ref.shape[0]):
            out_ref[s] = total[:, s * width : (s + 1) * width].astype(out_ref.dtype)


def begin(chan_index, field, table, group, parts):
    planes, cells = field.shape[1:]
    width = table.shape[1]
    rows = group * planes
    block = pick(cells, 1024)
    return pl.pallas_call(
        begin_kernel,
        grid_spec=pltpu.PrefetchScalarGridSpec(
            num_scalar_prefetch=1,
            grid=(cells // block,),
            in_specs=[
                pl.BlockSpec((group, planes, block), lambda s, chan: (chan[0], 0, s)),
                pl.BlockSpec((block, width), lambda s, chan: (s, 0)),
            ],
            out_specs=whole((parts, rows, width // parts)),
            scratch_shapes=[pltpu.VMEM((rows, width), jnp.float32)],
        ),
        out_shape=jax.ShapeDtypeStruct((parts, rows, width // parts), jnp.bfloat16),
        compiler_params=params(),
        cost_estimate=pl.CostEstimate(
            flops=2 * rows * cells * width,
            bytes_accessed=2 * cells * (width + rows),
            transcendentals=0,
        ),
        name="begin",
    )(chan_index.reshape(1), field, table)


def exchange_kernel(axes, sizes, blocks, *refs):
    count = len(blocks)
    ins, outs = refs[:count], refs[count : 2 * count]
    send, recv, local = refs[2 * count :]
    total = math.prod(sizes)
    last = sizes[-1]
    me = lax.axis_index(axes[0])
    if len(axes) == 2:
        me = me * last + lax.axis_index(axes[1])

    def place(index):
        if len(axes) == 2:
            return {axes[0]: lax.div(index, last), axes[1]: lax.rem(index, last)}
        return {axes[0]: index}

    def source(a, index):
        if blocks[a] == total:
            return ins[a].at[index]
        if blocks[a] == 1:
            return ins[a].at[0]
        return ins[a].at[lax.rem(index, last)]

    def copy(a, shift):
        peer = lax.rem(me + shift, total)
        return pltpu.make_async_remote_copy(
            src_ref=source(a, peer),
            dst_ref=outs[a].at[me],
            send_sem=send.at[a, shift],
            recv_sem=recv.at[a, shift],
            device_id=place(peer),
            device_id_type=pl.DeviceIdType.MESH,
        )

    barrier = pltpu.get_barrier_semaphore()

    def greet(shift, carry):
        pl.semaphore_signal(
            barrier, inc=1, device_id=place(lax.rem(me + shift, total)),
            device_id_type=pl.DeviceIdType.MESH,
        )
        return carry

    def start(shift, carry):
        for a in range(count):
            copy(a, shift).start()
        return carry

    def wait(shift, carry):
        for a in range(count):
            copy(a, shift).wait()
        return carry

    lax.fori_loop(1, total, greet, 0)
    own = [
        pltpu.make_async_copy(source(a, me), outs[a].at[me], local.at[a]) for a in range(count)
    ]
    for one in own:
        one.start()
    pl.semaphore_wait(barrier, total - 1)
    lax.fori_loop(1, total, start, 0)
    for one in own:
        one.wait()
    lax.fori_loop(1, total, wait, 0)


def exchange(arrays, axes, sizes, collective_id):
    total = math.prod(sizes)
    blocks = tuple(array.shape[0] for array in arrays)
    anywhere = pl.BlockSpec(memory_space=pl.ANY)
    return pl.pallas_call(
        functools.partial(exchange_kernel, axes, sizes, blocks),
        in_specs=[anywhere] * len(arrays),
        out_specs=[anywhere] * len(arrays),
        out_shape=[
            jax.ShapeDtypeStruct((total,) + array.shape[1:], array.dtype) for array in arrays
        ],
        scratch_shapes=[
            pltpu.SemaphoreType.DMA((len(arrays), total)),
            pltpu.SemaphoreType.DMA((len(arrays), total)),
            pltpu.SemaphoreType.DMA((len(arrays),)),
        ],
        compiler_params=pltpu.CompilerParams(
            collective_id=collective_id, has_side_effects=True, vmem_limit_bytes=VMEM_LIMIT
        ),
        cost_estimate=pl.CostEstimate(
            flops=0, bytes_accessed=sum(2 * a.size for a in arrays), transcendentals=0
        ),
        name="exchange",
    )(*arrays)


def pad_planes(array, dim, spare):
    if not spare:
        return array
    return jnp.pad(array, [(0, spare if d == dim else 0) for d in range(array.ndim)])


def body(slabs, chans, field, cotangent, spectral_weight, point_weight, point_bias):
    channels, planes, cells = field.shape
    group = spectral_weight.shape[1]
    modes = spectral_weight.shape[3]
    own_planes = -(-planes // chans)
    spare = own_planes * chans - planes
    length = planes * slabs
    width = 2 * modes
    tiled = planes % 16 == 0 and own_planes % 8 == 0 and width % 128 == 0
    everyone = ("slab", "chan"), (slabs, chans)
    table = lax.optimization_barrier(jnp.asarray(plane_table(slabs)))
    cosine, sine = line_tables(length)
    lines = jnp.asarray(np.concatenate([cosine, sine], 1))
    lines_back = jnp.asarray(np.concatenate([cosine.T, sine.T], 1))
    turn, turn_back = jnp.asarray(turned(modes)), jnp.asarray(turned(modes).T)
    part, pack = jnp.asarray(part_of(modes)), jnp.asarray(pack_of(modes))
    slab_index = lax.axis_index("slab")
    chan_index = lax.axis_index("chan")
    weight = jnp.swapaxes(spectral_weight, 3, 4)
    mode_index = slab_index * modes + jnp.arange(width, dtype=jnp.int32) % modes
    scale = (jnp.where(mode_index // MY == 0, 1.0, 2.0) / (length * cells)).astype(jnp.float32)
    scale = scale[None]

    if tiled:
        sections = begin(chan_index, field, table, group, slabs)
    else:
        own_field = lax.dynamic_slice_in_dim(field, chan_index * group, group, 0)
        sections = wide(own_field.reshape(group * planes, cells), table).astype(jnp.bfloat16)
        sections = jnp.moveaxis(sections.reshape(group * planes, slabs, width), 1, 0)
    (pencils,) = exchange([sections], ("slab",), (slabs,), 0)
    pencils = jnp.moveaxis(pencils.reshape(slabs, group, planes, width), 1, 0)
    partial, coeff = mix(
        pencils.reshape(group, length, width), lines, turn, part, pack, weight
    )
    (parts,) = exchange([partial.reshape(chans, group, MX, width)], ("chan",), (chans,), 1)
    pencils = spread(parts, scale, lines_back, turn_back)
    pencils = pad_planes(pencils.reshape(group, slabs, planes, width), 2, spare)
    pencils = pencils.reshape(group, slabs, chans, own_planes, width)
    pencils = jnp.transpose(pencils, (1, 2, 0, 3, 4))
    pencils = pencils.reshape(slabs * chans, group, own_planes, width)
    (slabs_in,) = exchange([pencils], *everyone, 4)
    slabs_in = slabs_in.reshape(slabs, channels, own_planes, width)
    rows = channels * own_planes
    slabs_in = jnp.transpose(slabs_in, (1, 2, 0, 3)).reshape(rows, slabs * width)

    own_index, own_field, own_cotangent = chan_index, field, cotangent
    if not tiled:
        own_index = jnp.zeros_like(chan_index)
        own_field, own_cotangent = (
            lax.dynamic_slice_in_dim(
                pad_planes(array, 1, spare), chan_index * own_planes, own_planes, 1
            )
            for array in (field, cotangent)
        )
    point, hat_rows, sums = grid_stage(
        own_index,
        slabs_in,
        table,
        own_field,
        own_cotangent,
        point_weight,
        jnp.repeat(point_bias.astype(jnp.float32), own_planes)[:, None],
        slabs if tiled else 1,
    )
    if not tiled:
        hat_rows = jnp.moveaxis(hat_rows.reshape(rows, slabs, width), 1, 0)
    hat_rows = hat_rows.reshape(slabs * chans, group, own_planes, width)
    own_sums = sums[:channels].reshape(chans, group, channels)
    bias_sums = jnp.broadcast_to(sums[channels:][None], (chans, 8, channels))
    own_sums = jnp.concatenate([own_sums, bias_sums], 1)
    pencils, all_sums = exchange([hat_rows, own_sums], *everyone, 2)
    pencils = jnp.moveaxis(pencils.reshape(slabs, chans, group, own_planes, width), 2, 0)
    pencils = pencils.reshape(group, slabs, chans * own_planes, width)[:, :, :planes]
    part_hat = gather_lines(pencils.reshape(group, length, width), scale, lines, turn)
    (hat,) = exchange([part_hat[None]], ("chan",), (chans,), 3)
    hat, point = lax.optimization_barrier((hat, point))
    point = point.reshape(chans, group, own_planes, cells)
    points = []
    for shift in range(chans):
        receiver = (chan_index + shift) % chans
        block = lax.dynamic_index_in_dim(point, receiver, 0, keepdims=False)
        if shift:
            block = lax.ppermute(block, "chan", [(c, (c + shift) % chans) for c in range(chans)])
        points.append(block)

    pencils, hat = adjoint_of(
        hat.reshape(channels, MX, width), lines_back, turn_back, part, pack, weight
    )
    pencils = pencils.reshape(group, slabs, planes, width)
    (pencils,) = exchange([jnp.moveaxis(pencils, 1, 0)], ("slab",), (slabs,), 5)
    grad_spectral = jnp.swapaxes(outer(coeff, hat), 3, 4)
    pencils = jnp.moveaxis(pencils, 0, 2).reshape(group * planes, slabs * width)
    if tiled:
        grad_input = finish(chan_index, pencils, table, points).reshape(group, planes, cells)
    else:
        back = lax.dot_general(pencils, table, ROWS_BY_ROWS, preferred_element_type=jnp.float32)
        back = back.reshape(group, planes, cells)
        order = (chan_index - jnp.arange(chans)) % chans
        point = jnp.take(jnp.stack(points), order, axis=0)
        point = jnp.moveaxis(point, 0, 1).reshape(group, chans * own_planes, cells)[:, :planes]
        grad_input = (back + point.astype(jnp.float32)).astype(jnp.bfloat16)

    sums = jnp.sum(all_sums, 0) * (1.0 / math.sqrt(length * cells))
    return (grad_input, grad_spectral, sums[:group], sums[group])


def solution(mesh):
    placed = (
        P(None, "slab", None),
        P(None, "slab", None),
        P(None, "chan", None, "slab", None),
        P(),
        P(),
    )
    return jax.shard_map(
        functools.partial(body, mesh.shape["slab"], mesh.shape["chan"]),
        mesh=mesh,
        in_specs=placed,
        out_specs=(
            P("chan", "slab", None),
            P(None, "chan", None, "slab", None),
            P("chan", None),
            P(),
        ),
        check_vma=False,
    )
```
